512 devices in a mesh: filt: 16 (over y, z_lo), space: 32 (over x, z_hi, core).
Axes of the slice: x: 4, y: 8, z: 8 (z_hi: 4, z_lo: 2; z = z_hi * 2 + z_lo), core: 2. Of those that a mesh axis runs over, the one named last changes fastest.
Arguments:
- activations: bfloat16 [128, 256, 8, 128], P('filt', 'space'), may hold values from -6 to 6
- cotangent: bfloat16 [128, 256, 8, 128], P('filt', 'space'), may hold values from -6 to 6
- filters: bfloat16 [27, 128, 128], P(None, 'filt'), may hold values from -0.109375 to 0.109375
- bias_terms: bfloat16 [128], P('filt'), may hold values from -3 to 3
Outputs:
- features_out: float32 [128, 256, 8, 128], P('filt', 'space')
- filter_grad: float32 [27, 128, 128], P(None, 'filt', 'space')
The draws below stay inside these ranges and needn't reach their ends.
All inputs are finite; a program needn't handle non-finite values.
Results may differ from the reference program's by a relative error of at most 0.0003.
Values may be sent and summed in bfloat16 or wider, within the bound.
No kernel may reach another device: no remote copies, remote signals or barrier semaphores. Data moves between devices by JAX's collectives and lax.ppermute only.
A program may use at most 128 MiB of HBM per device.

```python
import math
import jax
import jax.numpy as jnp
from jax import lax

CIN = 128
COUT = 128
TAPS = 27
Z = 8
Y = 128
NX = 256
NCELLS = 262144


def steps_of(rng, dims, cuts, smallest, high):
    def one(position, parts):
        draws = jax.random.uniform(jax.random.fold_in(jax.random.fold_in(rng, 6), position), (parts,), jnp.float32, smallest / len(cuts), high / len(cuts))
        return jnp.repeat(jnp.exp(draws), dims[position] // parts).reshape((-1,) + (1,) * (len(dims) - position - 1))

    gain = one(*cuts[0])
    for cut in cuts[1:]:
        gain = gain * one(*cut)
    return gain


def noise(rng, dims, spread, most, shards=(), dtype=jnp.bfloat16):
    values = jax.random.normal(rng, dims, jnp.float32) * spread
    if len(shards) > 0:
        values = steps_of(rng, dims, shards, -0.22, 0.18) * values
    return jnp.clip(values, min=-most, max=most).astype(dtype)


def setup_inputs(seed: int = 0) -> dict:
    streams_of = jax.random.split(jax.random.key(seed), 5)
    return {
        "activations": noise(streams_of[0], (CIN, NX, Z, Y), 1.0, 6.0, ((0, 16), (1, 32))),
        "cotangent": noise(streams_of[1], (COUT, NX, Z, Y), 1.0, 6.0, ((0, 16), (1, 32))),
        "filters": noise(streams_of[2], (TAPS, COUT, CIN), (CIN * TAPS) ** -0.5, 0.109375, ((1, 16),)),
        "bias_terms": noise(streams_of[3], (COUT,), 0.5, 3.0, ((0, 16),)),
    }


def tap_offsets(tap_index):
    return (tap_index // 9, tap_index // 3 % 3, tap_index % 3)

def reference(activations, cotangent, filters, bias_terms):
    padded = jnp.pad(activations.astype(jnp.float32), ((0, 0), (1, 1), (1, 1), (1, 1)))
    grad_in = cotangent.astype(jnp.float32)
    weights = filters.astype(jnp.float32)
    summed = jnp.zeros((COUT, NX, Z, Y), jnp.float32)
    grad_list = []
    for tap_index in range(TAPS):
        off_x, off_z, off_y = tap_offsets(tap_index)
        window = padded[:, off_x:off_x + NX, off_z:off_z + Z, off_y:off_y + Y]
        summed = summed + jnp.einsum('oi,ixzy->oxzy', weights[tap_index], window, precision=lax.Precision.HIGHEST)
        grad_list.append(jnp.einsum('oxzy,ixzy->oi', grad_in, window, precision=lax.Precision.HIGHEST))
    features_out = summed + bias_terms.astype(jnp.float32)[:, None, None, None]
    filter_grad = jnp.stack(grad_list) * jnp.float32(1.0 / math.sqrt(NCELLS))
    return (features_out, filter_grad)
```

```python
import functools
import math

import jax
import jax.numpy as jnp
from jax import lax
from jax.experimental import pallas as pl
from jax.experimental.pallas import tpu as pltpu
from jax.sharding import Mesh
from jax.sharding import PartitionSpec as P

SPACE = ("x", "zh", "core")
ROWS = 4
DEPTH = 8
WIDTH = 128
STEPS = 8


def local_kernel(place, b0, b1, b2, b3, b4a, b4b, b5, b6, b7, weights, cot, feat, grad):
    y = place[0]
    lane = lax.broadcasted_iota(jnp.int32, (16, WIDTH), 1)

    def block(j, row, z):
        if j == 4:
            return b4a[row, z] if row < 3 else b4b[row - 3, z]
        return (b0, b1, b2, b3, None, b5, b6, b7)[j][row, z]

    turned = pltpu.roll(
        weights[...].astype(jnp.float32).reshape(27 * 16, 128), lax.rem(128 - 16 * y, 128), 1
    ).astype(jnp.bfloat16)
    taps = jnp.concatenate(
        [
            jnp.concatenate(
                [turned[16 * (9 * dx + q) : 16 * (9 * dx + q) + 16] for q in range(9)], axis=0
            )
            for dx in range(3)
        ],
        axis=1,
    )

    total = jnp.zeros((384, 256), jnp.float32)
    gap = jnp.zeros((56, WIDTH), jnp.float32)
    empty = jnp.zeros((16, WIDTH), jnp.float32)
    for row in range(ROWS):
        cells = jnp.concatenate(
            [
                jnp.concatenate(
                    [block(j, row + dx, z) for dx in range(3) for j in range(STEPS)], axis=0
                )
                for z in range(DEPTH)
            ],
            axis=1,
        )
        part = jnp.dot(taps, cells, preferred_element_type=jnp.float32)
        for z in range(DEPTH):
            sums = []
            for dy in range(3):
                acc = None
                for dz in range(3):
                    if 0 <= z + dz - 1 < DEPTH:
                        at = 16 * (3 * dz + dy)
                        lo = WIDTH * (z + dz - 1)
                        term = part[at : at + 16, lo : lo + WIDTH]
                        acc = term if acc is None else acc + term
                sums.append(acc)
            left = jnp.where(lane == 0, 0.0, pltpu.roll(sums[0], 1, 1))
            right = jnp.where(lane == WIDTH - 1, 0.0, pltpu.roll(sums[2], WIDTH - 1, 1))
            feat[:, row, z, :] = sums[1] + left + right
        moved = []
        for z in range(DEPTH):
            here = cot[row, z].astype(jnp.float32)
            ahead = jnp.where(lane == WIDTH - 1, 0.0, pltpu.roll(here, WIDTH - 1, 1))
            behind = jnp.where(lane == 0, 0.0, pltpu.roll(here, 1, 1))
            moved.append((ahead, here, behind))
        spread = []
        for z in range(DEPTH):
            rows = []
            for half in range(2):
                for dz in range(3):
                    for dy in range(3):
                        at = z - dz + 1
                        tile = moved[at][dy] if 0 <= at < DEPTH else empty
                        rows.append(tile[8 * half : 8 * half + 8])
                rows.append(gap)
            spread.append(jnp.concatenate(rows, axis=0).astype(jnp.bfloat16))
        total = total + lax.dot_general(
            cells,
            jnp.concatenate(spread, axis=1),
            (((1,), (1,)), ((), ())),
            preferred_element_type=jnp.float32,
        )
    wide = lax.broadcasted_iota(jnp.int32, (128, WIDTH), 1)
    sub = lax.broadcasted_iota(jnp.int32, (8, WIDTH), 0)
    for half in range(2):
        one, two, three = (
            total[128 * dx : 128 * dx + 128, WIDTH * half : WIDTH * half + WIDTH]
            for dx in range(3)
        )
        one = jnp.where(wide < 72, one, pltpu.roll(three, 72, 1))
        two = jnp.where(wide < 72, two, pltpu.roll(three, 36, 1))
        for k in range(16):
            a, b = one[8 * k : 8 * k + 8], two[8 * k : 8 * k + 8]
            at = lax.rem(y + k // 2, STEPS) * 4 + 2 * (k % 2)
            grad[half, at] = jnp.where(sub < 4, a, pltpu.roll(b, 4, 0))
            grad[half, at + 1] = jnp.where(sub < 4, pltpu.roll(a, 4, 0), b)


def on_device(activations, cotangent, filters, bias_terms):
    y, zl = lax.axis_index("y"), lax.axis_index("zl")
    scale = jnp.float32(1.0 / math.sqrt(activations.shape[1] * 32 * DEPTH * WIDTH))
    acts = jnp.transpose(activations, (1, 2, 0, 3))
    cots = jnp.transpose(cotangent, (1, 2, 0, 3))
    first = zl == 0

    swap = [(0, 1), (1, 0)]
    other = lax.ppermute(lax.dynamic_slice_in_dim(acts, 3 * (1 - zl), 5, 0), "zl", swap)
    own = lax.dynamic_slice_in_dim(acts, 3 * zl, 5, 0)
    last, begin = acts[7:8], acts[0:1]
    pairs_own, pairs_other = [], []
    for s in range(31):
        pairs_own += [(s, s + 1), (32 + s + 1, 32 + s)]
        pairs_other += [(32 + s, s + 1), (s + 1, 32 + s)]
    axes = ("zl",) + SPACE
    edge_own = lax.ppermute(jnp.where(first, last, begin), axes, pairs_own)
    edge_other = lax.ppermute(jnp.where(first, begin, last), axes, pairs_other)

    def rows_of(body, edge):
        return jnp.where(
            first,
            jnp.concatenate([edge, body], axis=0),
            jnp.concatenate([body, edge], axis=0),
        )

    own, other = rows_of(own, edge_own), rows_of(other, edge_other)
    mine = jnp.where(
        first,
        jnp.concatenate([own, other], axis=2),
        jnp.concatenate([other, own], axis=2),
    )

    up = [(i, (i - 1) % STEPS) for i in range(STEPS)]
    down = [(i, (i + 1) % STEPS) for i in range(STEPS)]
    b1, b7 = lax.ppermute(mine, "y", up), lax.ppermute(mine, "y", down)
    b2, b6 = lax.ppermute(b1, "y", up), lax.ppermute(b7, "y", down)
    b3, b5 = lax.ppermute(b2, "y", up), lax.ppermute(b6, "y", down)
    b4a, b4b = lax.ppermute(b3[:3], "y", up), lax.ppermute(b5[3:], "y", down)

    give = jnp.concatenate(
        [lax.dynamic_slice_in_dim(cots, 4 * (1 - zl), 4, 0).reshape(32, 8, WIDTH), filters], axis=0
    )
    got = lax.ppermute(give, "zl", swap)
    keep = lax.dynamic_slice_in_dim(cots, 4 * zl, 4, 0)
    cot = jnp.concatenate([keep, got[:32].reshape(4, 8, 8, WIDTH)], axis=2)
    weights = jnp.concatenate([filters, got[32:]], axis=1)

    vmem = pl.BlockSpec(memory_space=pltpu.VMEM)
    feat, grad = pl.pallas_call(
        local_kernel,
        out_shape=(
            jax.ShapeDtypeStruct((16, ROWS, DEPTH, WIDTH), jnp.float32),
            jax.ShapeDtypeStruct((2, 32, 8, WIDTH), jnp.float32),
        ),
        in_specs=[pl.BlockSpec(memory_space=pltpu.SMEM)] + [vmem] * 11,
        out_specs=(vmem, vmem),
        compiler_params=pltpu.CompilerParams(vmem_limit_bytes=48 * 1024 * 1024),
        cost_estimate=pl.CostEstimate(flops=10**9, bytes_accessed=3 * 10**6, transcendentals=0),
    )(jnp.stack([y, zl]), mine, b1, b2, b3, b4a, b4b, b5, b6, b7, weights, cot)

    part = grad[0] + lax.ppermute(grad[1], "zl", swap)
    got = lax.all_to_all(part, SPACE, 0, 0, tiled=True)
    summed = jnp.sum(got, axis=0) * scale
    low, high = summed[:4], summed[4:]
    filter_grad = jnp.stack(
        [low[:, :72], high[:, :72], jnp.concatenate([low[:, 72:108], high[:, 72:108]], axis=1)]
    )
    filter_grad = filter_grad.reshape(3, 4, 9, 8).transpose(0, 2, 3, 1).reshape(27, 8, 4)

    rest = lax.ppermute(feat[8:], "zl", swap)
    kept = feat[:8]
    features_out = jnp.where(
        first,
        jnp.concatenate([kept, rest], axis=1),
        jnp.concatenate([rest, kept], axis=1),
    ) + bias_terms.astype(jnp.float32)[:, None, None, None]
    return (features_out, filter_grad)


def solution(mesh):
    fine = Mesh(mesh.devices.reshape(8, 2, 4, 4, 2), ("y", "zl", "x", "zh", "core"))
    filt = ("y", "zl")
    in_specs = (
        P(filt, SPACE, None, None),
        P(filt, SPACE, None, None),
        P(None, filt, None),
        P(filt),
    )
    out_specs = (P(filt, SPACE, None, None), P(None, filt, SPACE))
    return jax.shard_map(
        on_device, mesh=fine, in_specs=in_specs, out_specs=out_specs, check_vma=False
    )
```

```python
import functools
import math

import jax
import jax.numpy as jnp
from jax import lax
from jax.experimental import pallas as pl
from jax.experimental.pallas import tpu as pltpu
from jax.sharding import Mesh
from jax.sharding import PartitionSpec as P

SPACE = ("x", "zh", "core")
ROWS = 4
DEPTH = 8
WIDTH = 128
STEPS = 8


def block_of(blocks, j, row, z):
    b0, b1, b2, b3, b4a, b4b, b5, b6, b7 = blocks
    if j == 4:
        return b4a[row, z] if row < 3 else b4b[row - 3, z]
    return (b0, b1, b2, b3, None, b5, b6, b7)[j][row, z]


def cells_of(blocks, row):
    return jnp.concatenate(
        [
            jnp.concatenate(
                [block_of(blocks, j, row + dx, z) for dx in range(3) for j in range(STEPS)],
                axis=0,
            )
            for z in range(DEPTH)
        ],
        axis=1,
    )


def forward_kernel(place, *refs):
    *blocks, weights, feat = refs
    y = place[0]
    lane = lax.broadcasted_iota(jnp.int32, (16, WIDTH), 1)
    turned = pltpu.roll(
        weights[...].astype(jnp.float32).reshape(27 * 16, 128), lax.rem(128 - 16 * y, 128), 1
    ).astype(jnp.bfloat16)
    taps = jnp.concatenate(
        [
            jnp.concatenate(
                [turned[16 * (9 * dx + q) : 16 * (9 * dx + q) + 16] for q in range(9)], axis=0
            )
            for dx in range(3)
        ],
        axis=1,
    )
    for row in range(ROWS):
        part = jnp.dot(taps, cells_of(blocks, row), preferred_element_type=jnp.float32)
        for z in range(DEPTH):
            sums = []
            for dy in range(3):
                acc = None
                for dz in range(3):
                    if 0 <= z + dz - 1 < DEPTH:
                        at = 16 * (3 * dz + dy)
                        lo = WIDTH * (z + dz - 1)
                        term = part[at : at + 16, lo : lo + WIDTH]
                        acc = term if acc is None else acc + term
                sums.append(acc)
            left = jnp.where(lane == 0, 0.0, pltpu.roll(sums[0], 1, 1))
            right = jnp.where(lane == WIDTH - 1, 0.0, pltpu.roll(sums[2], WIDTH - 1, 1))
            feat[:, row, z, :] = sums[1] + left + right


def gradient_kernel(place, *refs):
    *blocks, cot, grad = refs
    y, zl = place[0], place[1]
    lane = lax.broadcasted_iota(jnp.int32, (16, WIDTH), 1)
    total = jnp.zeros((384, 256), jnp.float32)
    gap = jnp.zeros((56, WIDTH), jnp.float32)
    empty = jnp.zeros((16, WIDTH), jnp.float32)
    for row in range(ROWS):
        moved = []
        for z in range(DEPTH):
            here = cot[row, z].astype(jnp.float32)
            ahead = jnp.where(lane == WIDTH - 1, 0.0, pltpu.roll(here, WIDTH - 1, 1))
            behind = jnp.where(lane == 0, 0.0, pltpu.roll(here, 1, 1))
            moved.append((ahead, here, behind))
        spread = []
        for z in range(DEPTH):
            rows = []
            for half in range(2):
                for dz in range(3):
                    for dy in range(3):
                        at = z - dz + 1
                        tile = moved[at][dy] if 0 <= at < DEPTH else empty
                        rows.append(tile[8 * half : 8 * half + 8])
                rows.append(gap)
            spread.append(jnp.concatenate(rows, axis=0).astype(jnp.bfloat16))
        total = total + lax.dot_general(
            cells_of(blocks, row),
            jnp.concatenate(spread, axis=1),
            (((1,), (1,)), ((), ())),
            preferred_element_type=jnp.float32,
        )
    wide = lax.broadcasted_iota(jnp.int32, (128, WIDTH), 1)
    sub = lax.broadcasted_iota(jnp.int32, (8, WIDTH), 0)
    for half in range(2):
        one, two, three = (
            total[128 * dx : 128 * dx + 128, WIDTH * half : WIDTH * half + WIDTH]
            for dx in range(3)
        )
        one = jnp.where(wide < 72, one, pltpu.roll(three, 72, 1))
        two = jnp.where(wide < 72, two, pltpu.roll(three, 36, 1))
        base = 32 * lax.rem(zl + half, 2)
        for k in range(16):
            a, b = one[8 * k : 8 * k + 8], two[8 * k : 8 * k + 8]
            at = base + lax.rem(y + k // 2, STEPS) * 4 + 2 * (k % 2)
            grad[at] = jnp.where(sub < 4, a, pltpu.roll(b, 4, 0))
            grad[at + 1] = jnp.where(sub < 4, pltpu.roll(a, 4, 0), b)


def on_device(activations, cotangent, filters, bias_terms):
    y, zl = lax.axis_index("y"), lax.axis_index("zl")
    scale = jnp.float32(1.0 / math.sqrt(activations.shape[1] * 32 * DEPTH * WIDTH))
    acts = jnp.transpose(activations, (1, 2, 0, 3))
    cots = jnp.transpose(cotangent, (1, 2, 0, 3))
    first = zl == 0

    swap = [(0, 1), (1, 0)]
    other = lax.ppermute(lax.dynamic_slice_in_dim(acts, 3 * (1 - zl), 5, 0), "zl", swap)
    own = lax.dynamic_slice_in_dim(acts, 3 * zl, 5, 0)
    pairs = []
    for step in range(31):
        pairs += [(32 + step, step + 1), (step + 1, 32 + step)]

    body = jnp.where(
        first,
        jnp.concatenate([own, other], axis=2),
        jnp.concatenate([other, own], axis=2),
    )
    edge = lax.ppermute(jnp.where(first, body[0:1], body[4:5]), ("zl",) + SPACE, pairs)
    mine = jnp.where(
        first,
        jnp.concatenate([edge, body], axis=0),
        jnp.concatenate([body, edge], axis=0),
    )

    def along(block, by):
        return lax.ppermute(block, "y", [(i, (i - by) % STEPS) for i in range(STEPS)])

    b2, b6 = along(mine, 2), along(mine, -2)
    b1, b7 = along(mine, 1), along(mine, -1)
    b3, b5 = along(b2, 1), along(b6, -1)
    b4a, b4b = along(b2[:3], 2), along(b6[3:], -2)

    give = jnp.concatenate(
        [lax.dynamic_slice_in_dim(cots, 4 * (1 - zl), 4, 0).reshape(32, 8, WIDTH), filters], axis=0
    )
    got = lax.ppermute(give, "zl", swap)
    keep = lax.dynamic_slice_in_dim(cots, 4 * zl, 4, 0)
    cot = jnp.concatenate([keep, got[:32].reshape(4, 8, 8, WIDTH)], axis=2)
    weights = jnp.concatenate([filters, got[32:]], axis=1)

    blocks = (mine, b1, b2, b3, b4a, b4b, b5, b6, b7)
    place = jnp.stack([y, zl])
    vmem = pl.BlockSpec(memory_space=pltpu.VMEM)
    settings = dict(
        in_specs=[pl.BlockSpec(memory_space=pltpu.SMEM)] + [vmem] * 10,
        out_specs=vmem,
        compiler_params=pltpu.CompilerParams(vmem_limit_bytes=48 * 1024 * 1024),
        cost_estimate=pl.CostEstimate(flops=10**9, bytes_accessed=3 * 10**6, transcendentals=0),
    )
    grad = pl.pallas_call(
        gradient_kernel,
        out_shape=jax.ShapeDtypeStruct((64, 8, WIDTH), jnp.float32),
        **settings,
    )(place, *blocks, cot)
    feat = pl.pallas_call(
        forward_kernel,
        out_shape=jax.ShapeDtypeStruct((16, ROWS, DEPTH, WIDTH), jnp.float32),
        **settings,
    )(place, *blocks, weights)

    got = lax.all_to_all(grad, ("zl",) + SPACE, 0, 0, tiled=True)
    summed = jnp.sum(got, axis=0) * scale
    low, high = summed[:4], summed[4:]
    filter_grad = jnp.stack(
        [low[:, :72], high[:, :72], jnp.concatenate([low[:, 72:108], high[:, 72:108]], axis=1)]
    )
    filter_grad = filter_grad.reshape(3, 4, 9, 8).transpose(0, 2, 3, 1).reshape(27, 8, 4)

    rest = lax.ppermute(feat[8:], "zl", swap)
    kept = feat[:8]
    features_out = jnp.where(
        first,
        jnp.concatenate([kept, rest], axis=1),
        jnp.concatenate([rest, kept], axis=1),
    ) + bias_terms.astype(jnp.float32)[:, None, None, None]
    return (features_out, filter_grad)


def solution(mesh):
    fine = Mesh(mesh.devices.reshape(8, 2, 4, 4, 2), ("y", "zl", "x", "zh", "core"))
    filt = ("y", "zl")
    in_specs = (
        P(filt, SPACE, None, None),
        P(filt, SPACE, None, None),
        P(None, filt, None),
        P(filt),
    )
    out_specs = (P(filt, SPACE, None, None), P(None, filt, SPACE))
    return jax.shard_map(
        on_device, mesh=fine, in_specs=in_specs, out_specs=out_specs, check_vma=False
    )
```

```python
import functools
import math

import jax
import jax.numpy as jnp
from jax import lax
from jax.experimental import pallas as pl
from jax.experimental.pallas import tpu as pltpu
from jax.sharding import Mesh
from jax.sharding import PartitionSpec as P

SPACE = ("x", "zh", "core")
ROWS = 4
DEPTH = 8
WIDTH = 128
STEPS = 8


def cells_of(blocks, row):
    return jnp.concatenate(
        [
            jnp.concatenate(
                [blocks[j][row + dx, z] for dx in range(3) for j in range(STEPS)],
                axis=0,
            )
            for z in range(DEPTH)
        ],
        axis=1,
    )


def forward_kernel(place, *refs):
    *blocks, weights, feat = refs
    y = place[0]
    lane = lax.broadcasted_iota(jnp.int32, (16, WIDTH), 1)
    turned = pltpu.roll(
        weights[...].astype(jnp.float32).reshape(27 * 16, 128), lax.rem(128 - 16 * y, 128), 1
    ).astype(jnp.bfloat16)
    taps = jnp.concatenate(
        [
            jnp.concatenate(
                [turned[16 * (9 * dx + q) : 16 * (9 * dx + q) + 16] for q in range(9)], axis=0
            )
            for dx in range(3)
        ],
        axis=1,
    )
    for row in range(ROWS):
        part = jnp.dot(taps, cells_of(blocks, row), preferred_element_type=jnp.float32)
        for z in range(DEPTH):
            sums = []
            for dy in range(3):
                acc = None
                for dz in range(3):
                    if 0 <= z + dz - 1 < DEPTH:
                        at = 16 * (3 * dz + dy)
                        lo = WIDTH * (z + dz - 1)
                        term = part[at : at + 16, lo : lo + WIDTH]
                        acc = term if acc is None else acc + term
                sums.append(acc)
            left = jnp.where(lane == 0, 0.0, pltpu.roll(sums[0], 1, 1))
            right = jnp.where(lane == WIDTH - 1, 0.0, pltpu.roll(sums[2], WIDTH - 1, 1))
            feat[:, row, z, :] = sums[1] + left + right


def gradient_kernel(place, *refs):
    *blocks, cot, grad = refs
    y, zl = place[0], place[1]
    lane = lax.broadcasted_iota(jnp.int32, (16, WIDTH), 1)
    total = jnp.zeros((384, 256), jnp.float32)
    gap = jnp.zeros((56, WIDTH), jnp.float32)
    empty = jnp.zeros((16, WIDTH), jnp.float32)
    for row in range(ROWS):
        moved = []
        for z in range(DEPTH):
            here = cot[row, z].astype(jnp.float32)
            ahead = jnp.where(lane == WIDTH - 1, 0.0, pltpu.roll(here, WIDTH - 1, 1))
            behind = jnp.where(lane == 0, 0.0, pltpu.roll(here, 1, 1))
            moved.append((ahead, here, behind))
        spread = []
        for z in range(DEPTH):
            rows = []
            for half in range(2):
                for dz in range(3):
                    for dy in range(3):
                        at = z - dz + 1
                        tile = moved[at][dy] if 0 <= at < DEPTH else empty
                        rows.append(tile[8 * half : 8 * half + 8])
                rows.append(gap)
            spread.append(jnp.concatenate(rows, axis=0).astype(jnp.bfloat16))
        total = total + lax.dot_general(
            cells_of(blocks, row),
            jnp.concatenate(spread, axis=1),
            (((1,), (1,)), ((), ())),
            preferred_element_type=jnp.float32,
        )
    wide = lax.broadcasted_iota(jnp.int32, (128, WIDTH), 1)
    sub = lax.broadcasted_iota(jnp.int32, (8, WIDTH), 0)
    for half in range(2):
        one, two, three = (
            total[128 * dx : 128 * dx + 128, WIDTH * half : WIDTH * half + WIDTH]
            for dx in range(3)
        )
        one = jnp.where(wide < 72, one, pltpu.roll(three, 72, 1))
        two = jnp.where(wide < 72, two, pltpu.roll(three, 36, 1))
        base = 32 * lax.rem(zl + half, 2)
        for k in range(16):
            a, b = one[8 * k : 8 * k + 8], two[8 * k : 8 * k + 8]
            at = base + lax.rem(y + k // 2, STEPS) * 4 + 2 * (k % 2)
            grad[at] = jnp.where(sub < 4, a, pltpu.roll(b, 4, 0))
            grad[at + 1] = jnp.where(sub < 4, pltpu.roll(a, 4, 0), b)


def on_device(activations, cotangent, filters, bias_terms):
    y, zl = lax.axis_index("y"), lax.axis_index("zl")
    scale = jnp.float32(1.0 / math.sqrt(activations.shape[1] * 32 * DEPTH * WIDTH))
    acts = jnp.transpose(activations, (1, 2, 0, 3))
    cots = jnp.transpose(cotangent, (1, 2, 0, 3))
    first = zl == 0

    swap = [(0, 1), (1, 0)]
    other = lax.ppermute(lax.dynamic_slice_in_dim(acts, 3 * (1 - zl), 5, 0), "zl", swap)
    own = lax.dynamic_slice_in_dim(acts, 3 * zl, 5, 0)
    pairs = []
    for step in range(31):
        pairs += [(32 + step, step + 1), (step + 1, 32 + step)]

    body = jnp.where(
        first,
        jnp.concatenate([own, other], axis=2),
        jnp.concatenate([other, own], axis=2),
    )
    give = jnp.concatenate(
        [lax.dynamic_slice_in_dim(cots, 4 * (1 - zl), 4, 0).reshape(32, 8, WIDTH), filters], axis=0
    )
    got = lax.ppermute(give, "zl", swap)

    edge = lax.ppermute(jnp.where(first, body[0:1], body[4:5]), ("zl",) + SPACE, pairs)
    edge, got = lax.optimization_barrier((edge, got))
    mine = jnp.where(
        first,
        jnp.concatenate([edge, body], axis=0),
        jnp.concatenate([body, edge], axis=0),
    )

    def along(block, by):
        return lax.ppermute(block, "y", [(i, (i - by) % STEPS) for i in range(STEPS)])

    b2, b6 = along(mine, 2), along(mine, -2)
    b1, b7 = along(mine, 1), along(mine, -1)
    turn = [
        ((2 * i + c), (2 * ((i + (2 if c else -2)) % STEPS) + c))
        for i in range(STEPS)
        for c in range(2)
    ]
    b4 = lax.ppermute(jnp.where(lax.axis_index("core") == 0, b2, b6), ("y", "core"), turn)
    b3, b5 = along(b2, 1), along(b6, -1)

    keep = lax.dynamic_slice_in_dim(cots, 4 * zl, 4, 0)
    cot = jnp.concatenate([keep, got[:32].reshape(4, 8, 8, WIDTH)], axis=2)
    weights = jnp.concatenate([filters, got[32:]], axis=1)

    blocks = (mine, b1, b2, b3, b4, b5, b6, b7)
    place = jnp.stack([y, zl])
    vmem = pl.BlockSpec(memory_space=pltpu.VMEM)
    settings = dict(
        in_specs=[pl.BlockSpec(memory_space=pltpu.SMEM)] + [vmem] * 9,
        out_specs=vmem,
        compiler_params=pltpu.CompilerParams(vmem_limit_bytes=48 * 1024 * 1024),
        cost_estimate=pl.CostEstimate(flops=10**9, bytes_accessed=3 * 10**6, transcendentals=0),
    )
    grad = pl.pallas_call(
        gradient_kernel,
        out_shape=jax.ShapeDtypeStruct((64, 8, WIDTH), jnp.float32),
        **settings,
    )(place, *blocks, cot)
    feat = pl.pallas_call(
        forward_kernel,
        out_shape=jax.ShapeDtypeStruct((16, ROWS, DEPTH, WIDTH), jnp.float32),
        **settings,
    )(place, *blocks, weights)

    got = lax.all_to_all(grad, ("zl",) + SPACE, 0, 0, tiled=True)
    summed = jnp.sum(got, axis=0) * scale
    low, high = summed[:4], summed[4:]
    filter_grad = jnp.stack(
        [low[:, :72], high[:, :72], jnp.concatenate([low[:, 72:108], high[:, 72:108]], axis=1)]
    )
    filter_grad = filter_grad.reshape(3, 4, 9, 8).transpose(0, 2, 3, 1).reshape(27, 8, 4)

    rest = lax.ppermute(feat[8:], "zl", swap)
    kept = feat[:8]
    features_out = jnp.where(
        first,
        jnp.concatenate([kept, rest], axis=1),
        jnp.concatenate([rest, kept], axis=1),
    ) + bias_terms.astype(jnp.float32)[:, None, None, None]
    return (features_out, filter_grad)


def solution(mesh):
    fine = Mesh(mesh.devices.reshape(8, 2, 4, 4, 2), ("y", "zl", "x", "zh", "core"))
    filt = ("y", "zl")
    in_specs = (
        P(filt, SPACE, None, None),
        P(filt, SPACE, None, None),
        P(None, filt, None),
        P(filt),
    )
    out_specs = (P(filt, SPACE, None, None), P(None, filt, SPACE))
    return jax.shard_map(
        on_device, mesh=fine, in_specs=in_specs, out_specs=out_specs, check_vma=False
    )
```

```python
import functools
import math

import jax
import jax.numpy as jnp
from jax import lax
from jax.experimental import pallas as pl
from jax.experimental.pallas import tpu as pltpu
from jax.sharding import Mesh
from jax.sharding import PartitionSpec as P

SPACE = ("x", "zh", "core")
ROWS = 4
DEPTH = 8
WIDTH = 128
STEPS = 8


def fill(rows, place, blocks, edges):
    zl = place[1]
    for p, block in enumerate(blocks):
        rows[p, pl.ds(1 - zl, 5)] = block[...]
    at = 0
    for edge in edges:
        rows[pl.ds(at, edge.shape[0]), 5 * zl] = edge[...]
        at += edge.shape[0]


def cells_of(rows, count, row):
    return jnp.concatenate(
        [
            jnp.concatenate(
                [rows[p, row + dx, z] for dx in range(3) for p in range(count)], axis=0
            )
            for z in range(DEPTH)
        ],
        axis=1,
    )


def forward_kernel(place, *refs):
    *blocks, edge_a, edge_b, weights, feat, rows = refs
    y = place[0]
    fill(rows, place, blocks, (edge_a, edge_b))
    lane = lax.broadcasted_iota(jnp.int32, (16, WIDTH), 1)
    turned = pltpu.roll(
        weights[...].astype(jnp.float32).reshape(27 * 16, 128), lax.rem(128 - 16 * y + 32, 128), 1
    ).astype(jnp.bfloat16)
    taps = jnp.concatenate(
        [
            jnp.concatenate(
                [turned[16 * (9 * dx + q) : 16 * (9 * dx + q) + 16] for q in range(9)], axis=0
            )
            for dx in range(3)
        ],
        axis=1,
    )
    for row in range(ROWS):
        part = jnp.dot(taps, cells_of(rows, STEPS, row), preferred_element_type=jnp.float32)
        for z in range(DEPTH):
            sums = []
            for dy in range(3):
                acc = None
                for dz in range(3):
                    if 0 <= z + dz - 1 < DEPTH:
                        at = 16 * (3 * dz + dy)
                        lo = WIDTH * (z + dz - 1)
                        term = part[at : at + 16, lo : lo + WIDTH]
                        acc = term if acc is None else acc + term
                sums.append(acc)
            left = jnp.where(lane == 0, 0.0, pltpu.roll(sums[0], 1, 1))
            right = jnp.where(lane == WIDTH - 1, 0.0, pltpu.roll(sums[2], WIDTH - 1, 1))
            feat[:, row, z, :] = sums[1] + left + right


def gradient_kernel(skip, count, place, *refs):
    blocks, (edge, cot, *earlier, grad, rows) = refs[:count], refs[count:]
    y, zl = place[0], place[1]
    for part in earlier:
        grad[...] = part[...]
    fill(rows, place, blocks, (edge,))
    lane = lax.broadcasted_iota(jnp.int32, (16, WIDTH), 1)
    total = jnp.zeros((48 * count, 256), jnp.float32)
    gap = jnp.zeros((56, WIDTH), jnp.float32)
    empty = jnp.zeros((16, WIDTH), jnp.float32)
    for row in range(ROWS):
        moved = []
        for z in range(DEPTH):
            here = cot[row, z].astype(jnp.float32)
            ahead = jnp.where(lane == WIDTH - 1, 0.0, pltpu.roll(here, WIDTH - 1, 1))
            behind = jnp.where(lane == 0, 0.0, pltpu.roll(here, 1, 1))
            moved.append((ahead, here, behind))
        spread = []
        for z in range(DEPTH):
            column = []
            for half in range(2):
                for dz in range(3):
                    for dy in range(3):
                        at = z - dz + 1
                        tile = moved[at][dy] if 0 <= at < DEPTH else empty
                        column.append(tile[8 * half : 8 * half + 8])
                column.append(gap)
            spread.append(jnp.concatenate(column, axis=0).astype(jnp.bfloat16))
        total = total + lax.dot_general(
            cells_of(rows, count, row),
            jnp.concatenate(spread, axis=1),
            (((1,), (1,)), ((), ())),
            preferred_element_type=jnp.float32,
        )
    deep = 16 * count
    wide = lax.broadcasted_iota(jnp.int32, (deep, WIDTH), 1)
    sub = lax.broadcasted_iota(jnp.int32, (8, WIDTH), 0)
    for half in range(2):
        one, two, three = (
            total[deep * dx : deep * dx + deep, WIDTH * half : WIDTH * half + WIDTH]
            for dx in range(3)
        )
        one = jnp.where(wide < 72, one, pltpu.roll(three, 72, 1))
        two = jnp.where(wide < 72, two, pltpu.roll(three, 36, 1))
        base = 32 * lax.rem(zl + half, 2)
        for k in range(2 * count):
            a, b = one[8 * k : 8 * k + 8], two[8 * k : 8 * k + 8]
            at = base + lax.rem(y + skip + k // 2 + 6, STEPS) * 4 + 2 * (k % 2)
            grad[at] = jnp.where(sub < 4, a, pltpu.roll(b, 4, 0))
            grad[at + 1] = jnp.where(sub < 4, pltpu.roll(a, 4, 0), b)


def on_device(activations, cotangent, filters, bias_terms):
    y, zl = lax.axis_index("y"), lax.axis_index("zl")
    scale = jnp.float32(1.0 / math.sqrt(activations.shape[1] * 32 * DEPTH * WIDTH))
    acts = jnp.transpose(activations, (1, 2, 0, 3))
    cots = jnp.transpose(cotangent, (1, 2, 0, 3))
    first = zl == 0

    swap = [(0, 1), (1, 0)]
    other = lax.ppermute(lax.dynamic_slice_in_dim(acts, 3 * (1 - zl), 5, 0), "zl", swap)
    own = lax.dynamic_slice_in_dim(acts, 3 * zl, 5, 0)
    pairs = []
    for step in range(31):
        pairs += [(32 + step, step + 1), (step + 1, 32 + step)]

    mine = jnp.where(
        first,
        jnp.concatenate([own, other], axis=2),
        jnp.concatenate([other, own], axis=2),
    )
    give = jnp.concatenate(
        [lax.dynamic_slice_in_dim(cots, 4 * (1 - zl), 4, 0).reshape(32, 8, WIDTH), filters], axis=0
    )
    got = lax.ppermute(give, "zl", swap)

    def along(block, by):
        return lax.ppermute(block, "y", [(i, (i - by) % STEPS) for i in range(STEPS)])

    b2, b6 = along(mine, 2), along(mine, -2)
    after, got = lax.optimization_barrier((mine, got))
    b1, b7 = along(after, 1), along(after, -1)
    turn = [
        ((2 * i + c), (2 * ((i + (2 if c else -2)) % STEPS) + c))
        for i in range(STEPS)
        for c in range(2)
    ]
    b4 = lax.ppermute(jnp.where(lax.axis_index("core") == 0, b2, b6), ("y", "core"), turn)
    b3, b5 = along(b2, 1), along(b6, -1)

    def outermost(blocks):
        return jnp.stack([jnp.where(first, block[0], block[4]) for block in blocks])

    near = (b6, b7, mine, b1, b2)
    send, b3 = lax.optimization_barrier((outermost(near), b3))
    far = (b3, b4, b5)
    edge_a = lax.ppermute(send, ("zl",) + SPACE, pairs)
    edge_b = lax.ppermute(outermost(far), ("zl",) + SPACE, pairs)

    keep = lax.dynamic_slice_in_dim(cots, 4 * zl, 4, 0)
    cot = jnp.concatenate([keep, got[:32].reshape(4, 8, 8, WIDTH)], axis=2)
    weights = jnp.concatenate([filters, got[32:]], axis=1)

    place = jnp.stack([y, zl])

    def local(kernel, shape, blocks, *others):
        vmem = pl.BlockSpec(memory_space=pltpu.VMEM)
        return pl.pallas_call(
            kernel,
            out_shape=jax.ShapeDtypeStruct(shape, jnp.float32),
            in_specs=[pl.BlockSpec(memory_space=pltpu.SMEM)]
            + [vmem] * (len(blocks) + len(others)),
            out_specs=vmem,
            scratch_shapes=[pltpu.VMEM((len(blocks), 6, DEPTH, 16, WIDTH), jnp.bfloat16)],
            compiler_params=pltpu.CompilerParams(vmem_limit_bytes=48 * 1024 * 1024),
            cost_estimate=pl.CostEstimate(
                flops=10**8 * len(blocks), bytes_accessed=3 * 10**6, transcendentals=0
            ),
        )(place, *blocks, *others)

    tiles = (64, 8, WIDTH)
    grad = local(functools.partial(gradient_kernel, 0, 5), tiles, near, edge_a, cot)
    grad = local(functools.partial(gradient_kernel, 5, 3), tiles, far, edge_b, cot, grad)
    feat = local(
        forward_kernel, (16, ROWS, DEPTH, WIDTH), near + far, edge_a, edge_b, weights
    )

    got = lax.all_to_all(grad, ("zl",) + SPACE, 0, 0, tiled=True)
    summed = jnp.sum(got, axis=0) * scale
    low, high = summed[:4], summed[4:]
    filter_grad = jnp.stack(
        [low[:, :72], high[:, :72], jnp.concatenate([low[:, 72:108], high[:, 72:108]], axis=1)]
    )
    filter_grad = filter_grad.reshape(3, 4, 9, 8).transpose(0, 2, 3, 1).reshape(27, 8, 4)

    rest = lax.ppermute(feat[8:], "zl", swap)
    kept = feat[:8]
    features_out = jnp.where(
        first,
        jnp.concatenate([kept, rest], axis=1),
        jnp.concatenate([rest, kept], axis=1),
    ) + bias_terms.astype(jnp.float32)[:, None, None, None]
    return (features_out, filter_grad)


def solution(mesh):
    fine = Mesh(mesh.devices.reshape(8, 2, 4, 4, 2), ("y", "zl", "x", "zh", "core"))
    filt = ("y", "zl")
    in_specs = (
        P(filt, SPACE, None, None),
        P(filt, SPACE, None, None),
        P(None, filt, None),
        P(filt),
    )
    out_specs = (P(filt, SPACE, None, None), P(None, filt, SPACE))
    return jax.shard_map(
        on_device, mesh=fine, in_specs=in_specs, out_specs=out_specs, check_vma=False
    )
```

```python
import math

import jax
import jax.numpy as jnp
from jax import lax
from jax.experimental import pallas as pl
from jax.experimental.pallas import tpu as pltpu
from jax.sharding import Mesh
from jax.sharding import PartitionSpec as P

SPACE = ("x", "zh", "core")
ROWS = 4
DEPTH = 8
WIDTH = 128
STEPS = 8


def fill(rows, place, blocks, edge):
    zl = place[1]
    for p, block in enumerate(blocks):
        rows[p, pl.ds(1 - zl, 5)] = block[...]
    rows[:, 5 * zl] = edge


def cells_of(rows, row):
    return jnp.concatenate(
        [
            jnp.concatenate(
                [rows[p, row + dx, z] for dx in range(3) for p in range(STEPS)], axis=0
            )
            for z in range(DEPTH)
        ],
        axis=1,
    )


def forward_kernel(place, *refs):
    *blocks, edge, weights, feat, rows = refs
    y = place[0]
    fill(rows, place, blocks, edge[...])
    lane = lax.broadcasted_iota(jnp.int32, (16, WIDTH), 1)
    turned = pltpu.roll(
        weights[...].astype(jnp.float32).reshape(27 * 16, 128), lax.rem(128 - 16 * y + 32, 128), 1
    ).astype(jnp.bfloat16)
    taps = jnp.concatenate(
        [
            jnp.concatenate(
                [turned[16 * (9 * dx + q) : 16 * (9 * dx + q) + 16] for q in range(9)], axis=0
            )
            for dx in range(3)
        ],
        axis=1,
    )
    for row in range(ROWS):
        part = jnp.dot(taps, cells_of(rows, row), preferred_element_type=jnp.float32)
        for z in range(DEPTH):
            sums = []
            for dy in range(3):
                acc = None
                for dz in range(3):
                    if 0 <= z + dz - 1 < DEPTH:
                        at = 16 * (3 * dz + dy)
                        lo = WIDTH * (z + dz - 1)
                        term = part[at : at + 16, lo : lo + WIDTH]
                        acc = term if acc is None else acc + term
                sums.append(acc)
            left = jnp.where(lane == 0, 0.0, pltpu.roll(sums[0], 1, 1))
            right = jnp.where(lane == WIDTH - 1, 0.0, pltpu.roll(sums[2], WIDTH - 1, 1))
            feat[:, row, z, :] = sums[1] + left + right


def shifted(cot, row):
    lane = lax.broadcasted_iota(jnp.int32, (16, WIDTH), 1)
    gap = jnp.zeros((56, WIDTH), jnp.float32)
    empty = jnp.zeros((16, WIDTH), jnp.float32)
    moved = []
    for z in range(DEPTH):
        here = cot[row, z].astype(jnp.float32)
        ahead = jnp.where(lane == WIDTH - 1, 0.0, pltpu.roll(here, WIDTH - 1, 1))
        behind = jnp.where(lane == 0, 0.0, pltpu.roll(here, 1, 1))
        moved.append((ahead, here, behind))
    columns = []
    for z in range(DEPTH):
        column = []
        for half in range(2):
            for dz in range(3):
                for dy in range(3):
                    at = z - dz + 1
                    tile = moved[at][dy] if 0 <= at < DEPTH else empty
                    column.append(tile[8 * half : 8 * half + 8])
            column.append(gap)
        columns.append(jnp.concatenate(column, axis=0).astype(jnp.bfloat16))
    return jnp.concatenate(columns, axis=1)


def over_cells(a, b):
    return lax.dot_general(a, b, (((1,), (1,)), ((), ())), preferred_element_type=jnp.float32)


def receivers(place, half):
    y, zl = place[0], place[1]
    base = 32 * lax.rem(zl + half, 2)
    return [base + lax.rem(y + k // 2 + 6, STEPS) * 4 + 2 * (k % 2) for k in range(16)]


def pair_of(one, two, k):
    sub = lax.broadcasted_iota(jnp.int32, (8, WIDTH), 0)
    a, b = one[8 * k : 8 * k + 8], two[8 * k : 8 * k + 8]
    return jnp.where(sub < 4, a, pltpu.roll(b, 4, 0)), jnp.where(sub < 4, pltpu.roll(a, 4, 0), b)


def gradient_kernel(place, *refs):
    *blocks, cot, grad, rows = refs
    fill(rows, place, blocks, jnp.zeros((STEPS, DEPTH, 16, WIDTH), jnp.bfloat16))
    total = jnp.zeros((384, 256), jnp.float32)
    for row in range(ROWS):
        total = total + over_cells(cells_of(rows, row), shifted(cot, row))
    wide = lax.broadcasted_iota(jnp.int32, (128, WIDTH), 1)
    for half in range(2):
        one, two, three = (
            total[128 * dx : 128 * dx + 128, WIDTH * half : WIDTH * half + WIDTH]
            for dx in range(3)
        )
        one = jnp.where(wide < 72, one, pltpu.roll(three, 72, 1))
        two = jnp.where(wide < 72, two, pltpu.roll(three, 36, 1))
        for k, at in enumerate(receivers(place, half)):
            grad[at], grad[at + 1] = pair_of(one, two, k)


def edge_kernel(place, edge, cot, earlier, grad):
    zl = place[1]
    cells = jnp.concatenate(
        [jnp.concatenate([edge[p, z] for p in range(STEPS)], axis=0) for z in range(DEPTH)], axis=1
    )
    total = over_cells(cells, shifted(cot, 3 * zl))
    wide = lax.broadcasted_iota(jnp.int32, (128, WIDTH), 1)
    low = zl == 0
    for half in range(2):
        part = total[:, WIDTH * half : WIDTH * half + WIDTH]
        one = jnp.where(low, part, jnp.where(wide < 72, 0.0, pltpu.roll(part, 72, 1)))
        two = jnp.where(
            jnp.logical_or(low, wide < 72), 0.0, pltpu.roll(part, 36, 1)
        )
        for k, at in enumerate(receivers(place, half)):
            first, second = pair_of(one, two, k)
            grad[at] = earlier[at] + first
            grad[at + 1] = earlier[at + 1] + second


def on_device(activations, cotangent, filters, bias_terms):
    y, zl = lax.axis_index("y"), lax.axis_index("zl")
    scale = jnp.float32(1.0 / math.sqrt(activations.shape[1] * 32 * DEPTH * WIDTH))
    acts = jnp.transpose(activations, (1, 2, 0, 3))
    cots = jnp.transpose(cotangent, (1, 2, 0, 3))
    first = zl == 0

    swap = [(0, 1), (1, 0)]
    other = lax.ppermute(lax.dynamic_slice_in_dim(acts, 3 * (1 - zl), 5, 0), "zl", swap)
    own = lax.dynamic_slice_in_dim(acts, 3 * zl, 5, 0)
    pairs = []
    for step in range(31):
        pairs += [(32 + step, step + 1), (step + 1, 32 + step)]

    mine = jnp.where(
        first,
        jnp.concatenate([own, other], axis=2),
        jnp.concatenate([other, own], axis=2),
    )
    give = jnp.concatenate(
        [lax.dynamic_slice_in_dim(cots, 4 * (1 - zl), 4, 0).reshape(32, 8, WIDTH), filters], axis=0
    )
    got = lax.ppermute(give, "zl", swap)

    def along(block, by):
        return lax.ppermute(block, "y", [(i, (i - by) % STEPS) for i in range(STEPS)])

    b2, b6 = along(mine, 2), along(mine, -2)
    keep = lax.dynamic_slice_in_dim(cots, 4 * zl, 4, 0)
    cot = jnp.concatenate([keep, got[:32].reshape(4, 8, 8, WIDTH)], axis=2)
    weights = jnp.concatenate([filters, got[32:]], axis=1)
    after, cot, weights = lax.optimization_barrier((mine, cot, weights))
    b1, b7 = along(after, 1), along(after, -1)
    turn = [
        ((2 * i + c), (2 * ((i + (2 if c else -2)) % STEPS) + c))
        for i in range(STEPS)
        for c in range(2)
    ]
    b4 = lax.ppermute(jnp.where(lax.axis_index("core") == 0, b2, b6), ("y", "core"), turn)
    b3, b5 = along(b2, 1), along(b6, -1)

    blocks = (b6, b7, mine, b1, b2, b3, b4, b5)
    edge = lax.ppermute(
        jnp.stack([jnp.where(first, block[0], block[4]) for block in blocks]),
        ("zl",) + SPACE,
        pairs,
    )

    place = jnp.stack([y, zl])

    def local(kernel, shape, operands, scratch):
        vmem = pl.BlockSpec(memory_space=pltpu.VMEM)
        return pl.pallas_call(
            kernel,
            out_shape=jax.ShapeDtypeStruct(shape, jnp.float32),
            in_specs=[pl.BlockSpec(memory_space=pltpu.SMEM)] + [vmem] * len(operands),
            out_specs=vmem,
            scratch_shapes=scratch,
            compiler_params=pltpu.CompilerParams(vmem_limit_bytes=48 * 1024 * 1024),
            cost_estimate=pl.CostEstimate(
                flops=10**8 * len(operands), bytes_accessed=3 * 10**6, transcendentals=0
            ),
        )(place, *operands)

    tiles = (64, 8, WIDTH)
    rows = [pltpu.VMEM((STEPS, 6, DEPTH, 16, WIDTH), jnp.bfloat16)]
    grad = local(gradient_kernel, tiles, (*blocks, cot), rows)
    grad = local(edge_kernel, tiles, (edge, cot, grad), [])
    feat = local(forward_kernel, (16, ROWS, DEPTH, WIDTH), (*blocks, edge, weights), rows)

    got = lax.all_to_all(grad, ("zl",) + SPACE, 0, 0, tiled=True)
    summed = jnp.sum(got, axis=0) * scale
    low, high = summed[:4], summed[4:]
    filter_grad = jnp.stack(
        [low[:, :72], high[:, :72], jnp.concatenate([low[:, 72:108], high[:, 72:108]], axis=1)]
    )
    filter_grad = filter_grad.reshape(3, 4, 9, 8).transpose(0, 2, 3, 1).reshape(27, 8, 4)

    rest = lax.ppermute(feat[8:], "zl", swap)
    kept = feat[:8]
    features_out = jnp.where(
        first,
        jnp.concatenate([kept, rest], axis=1),
        jnp.concatenate([rest, kept], axis=1),
    ) + bias_terms.astype(jnp.float32)[:, None, None, None]
    return (features_out, filter_grad)


def solution(mesh):
    fine = Mesh(mesh.devices.reshape(8, 2, 4, 4, 2), ("y", "zl", "x", "zh", "core"))
    filt = ("y", "zl")
    in_specs = (
        P(filt, SPACE, None, None),
        P(filt, SPACE, None, None),
        P(None, filt, None),
        P(filt),
    )
    out_specs = (P(filt, SPACE, None, None), P(None, filt, SPACE))
    return jax.shard_map(
        on_device, mesh=fine, in_specs=in_specs, out_specs=out_specs, check_vma=False
    )
```

```python
import math

import jax
import jax.numpy as jnp
from jax import lax
from jax.experimental import pallas as pl
from jax.experimental.pallas import tpu as pltpu
from jax.sharding import Mesh
from jax.sharding import PartitionSpec as P

SPACE = ("x", "zh", "core")
ROWS = 4
DEPTH = 8
WIDTH = 128
STEPS = 8
SCALE = 1.0 / math.sqrt(256 * DEPTH * WIDTH)


def fill(rows, place, blocks, edges):
    zl = place[1]
    for p, block in enumerate(blocks):
        rows[p, pl.ds(1 - zl, 5)] = block[...]
    rows[0:5, 5 * zl] = edges[0]
    rows[5:8, 5 * zl] = edges[1]


def cells_of(rows, row):
    return jnp.concatenate(
        [
            jnp.concatenate(
                [rows[p, row + dx, z] for dx in range(3) for p in range(STEPS)], axis=0
            )
            for z in range(DEPTH)
        ],
        axis=1,
    )


def forward_kernel(place, *refs):
    *blocks, near, far, weights, feat, rows = refs
    y = place[0]
    fill(rows, place, blocks, (near[...], far[...]))
    lane = lax.broadcasted_iota(jnp.int32, (16, WIDTH), 1)
    turned = pltpu.roll(
        weights[...].astype(jnp.float32).reshape(27 * 16, 128), lax.rem(128 - 16 * y + 32, 128), 1
    ).astype(jnp.bfloat16)
    taps = jnp.concatenate(
        [
            jnp.concatenate(
                [turned[16 * (9 * dx + q) : 16 * (9 * dx + q) + 16] for q in range(9)], axis=0
            )
            for dx in range(3)
        ],
        axis=1,
    )
    for row in range(ROWS):
        part = jnp.dot(taps, cells_of(rows, row), preferred_element_type=jnp.float32)
        for z in range(DEPTH):
            sums = []
            for dy in range(3):
                acc = None
                for dz in range(3):
                    if 0 <= z + dz - 1 < DEPTH:
                        at = 16 * (3 * dz + dy)
                        lo = WIDTH * (z + dz - 1)
                        term = part[at : at + 16, lo : lo + WIDTH]
                        acc = term if acc is None else acc + term
                sums.append(acc)
            left = jnp.where(lane == 0, 0.0, pltpu.roll(sums[0], 1, 1))
            right = jnp.where(lane == WIDTH - 1, 0.0, pltpu.roll(sums[2], WIDTH - 1, 1))
            feat[:, row, z, :] = sums[1] + left + right


def shifted(cot, row):
    lane = lax.broadcasted_iota(jnp.int32, (16, WIDTH), 1)
    gap = jnp.zeros((56, WIDTH), jnp.float32)
    empty = jnp.zeros((16, WIDTH), jnp.float32)
    moved = []
    for z in range(DEPTH):
        here = cot[row, z].astype(jnp.float32)
        ahead = jnp.where(lane == WIDTH - 1, 0.0, pltpu.roll(here, WIDTH - 1, 1))
        behind = jnp.where(lane == 0, 0.0, pltpu.roll(here, 1, 1))
        moved.append((ahead, here, behind))
    columns = []
    for z in range(DEPTH):
        column = []
        for half in range(2):
            for dz in range(3):
                for dy in range(3):
                    at = z - dz + 1
                    tile = moved[at][dy] if 0 <= at < DEPTH else empty
                    column.append(tile[8 * half : 8 * half + 8])
            column.append(gap)
        columns.append(jnp.concatenate(column, axis=0).astype(jnp.bfloat16))
    return jnp.concatenate(columns, axis=1)


def edge_cells(near, far):
    return jnp.concatenate(
        [
            jnp.concatenate(
                [near[p, z] for p in range(5)] + [far[p, z] for p in range(3)], axis=0
            )
            for z in range(DEPTH)
        ],
        axis=1,
    )


def over_cells(a, b):
    return lax.dot_general(a, b, (((1,), (1,)), ((), ())), preferred_element_type=jnp.float32)


def receivers(place, half):
    y, zl = place[0], place[1]
    base = 32 * lax.rem(zl + half, 2)
    return [base + lax.rem(y + k // 2 + 6, STEPS) * 4 + 2 * (k % 2) for k in range(16)]


def pair_of(one, two, k):
    sub = lax.broadcasted_iota(jnp.int32, (8, WIDTH), 0)
    a, b = one[8 * k : 8 * k + 8], two[8 * k : 8 * k + 8]
    return jnp.where(sub < 4, a, pltpu.roll(b, 4, 0)), jnp.where(sub < 4, pltpu.roll(a, 4, 0), b)


def gradient_kernel(place, *refs):
    *blocks, cot, grad, moved, rows = refs
    zeros = [jnp.zeros((count, DEPTH, 16, WIDTH), jnp.bfloat16) for count in (5, 3)]
    fill(rows, place, blocks, zeros)
    total = jnp.zeros((384, 256), jnp.float32)
    for row in range(ROWS):
        here = shifted(cot, row)
        if row in (0, 3):
            moved[row // 3] = here
        total = total + over_cells(cells_of(rows, row), here)
    wide = lax.broadcasted_iota(jnp.int32, (128, WIDTH), 1)
    for half in range(2):
        one, two, three = (
            total[128 * dx : 128 * dx + 128, WIDTH * half : WIDTH * half + WIDTH]
            for dx in range(3)
        )
        one = jnp.where(wide < 72, one, pltpu.roll(three, 72, 1))
        two = jnp.where(wide < 72, two, pltpu.roll(three, 32, 1))
        for k, at in enumerate(receivers(place, half)):
            grad[at], grad[at + 1] = pair_of(one, two, k)


def edge_kernel(place, near, far, moved, earlier, grad):
    zl = place[1]
    total = over_cells(edge_cells(near, far), moved[zl])
    wide = lax.broadcasted_iota(jnp.int32, (128, WIDTH), 1)
    low = zl == 0
    for half in range(2):
        part = total[:, WIDTH * half : WIDTH * half + WIDTH]
        one = jnp.where(low, part, jnp.where(wide < 72, 0.0, pltpu.roll(part, 72, 1)))
        two = jnp.where(
            jnp.logical_or(low, wide < 72), 0.0, pltpu.roll(part, 32, 1)
        )
        for k, at in enumerate(receivers(place, half)):
            first, second = pair_of(one, two, k)
            grad[at] = earlier[at] + first
            grad[at + 1] = earlier[at + 1] + second


def finish_kernel(place, got, out):
    summed = jnp.transpose(jnp.sum(got[...], axis=0) * SCALE)
    for at, count, lane, start in ((0, 9, 0, 0), (9, 9, 4, 0), (18, 5, 0, 72), (23, 4, 4, 72)):
        part = summed[start : start + 8 * count, lane : lane + 4]
        out[at : at + count] = part.reshape(count, 8, 4)


def on_device(activations, cotangent, filters, bias_terms):
    y, zl = lax.axis_index("y"), lax.axis_index("zl")
    acts = jnp.transpose(activations, (1, 2, 0, 3))
    cots = jnp.transpose(cotangent, (1, 2, 0, 3))
    first = zl == 0

    swap = [(0, 1), (1, 0)]
    other = lax.ppermute(lax.dynamic_slice_in_dim(acts, 3 * (1 - zl), 5, 0), "zl", swap)
    own = lax.dynamic_slice_in_dim(acts, 3 * zl, 5, 0)
    pairs = []
    for step in range(31):
        pairs += [(32 + step, step + 1), (step + 1, 32 + step)]

    mine = jnp.where(
        first,
        jnp.concatenate([own, other], axis=2),
        jnp.concatenate([other, own], axis=2),
    )
    give = jnp.concatenate(
        [lax.dynamic_slice_in_dim(cots, 4 * (1 - zl), 4, 0).reshape(32, 8, WIDTH), filters], axis=0
    )
    got = lax.ppermute(give, "zl", swap)

    def along(block, by):
        return lax.ppermute(block, "y", [(i, (i - by) % STEPS) for i in range(STEPS)])

    b2, b6 = along(mine, 2), along(mine, -2)
    keep = lax.dynamic_slice_in_dim(cots, 4 * zl, 4, 0)
    cot = jnp.concatenate([keep, got[:32].reshape(4, 8, 8, WIDTH)], axis=2)
    weights = jnp.concatenate([filters, got[32:]], axis=1)
    after, cot, weights = lax.optimization_barrier((mine, cot, weights))
    b1, b7 = along(after, 1), along(after, -1)
    turn = [
        ((2 * i + c), (2 * ((i + (2 if c else -2)) % STEPS) + c))
        for i in range(STEPS)
        for c in range(2)
    ]
    b4 = lax.ppermute(jnp.where(lax.axis_index("core") == 0, b2, b6), ("y", "core"), turn)
    b3, b5 = along(b2, 1), along(b6, -1)

    def outermost(blocks):
        return jnp.stack([jnp.where(first, block[0], block[4]) for block in blocks])

    near = (b6, b7, mine, b1, b2)
    send, b3 = lax.optimization_barrier((outermost(near), b3))
    far = (b3, b4, b5)
    edges = (
        lax.ppermute(send, ("zl",) + SPACE, pairs),
        lax.ppermute(outermost(far), ("zl",) + SPACE, pairs),
    )
    blocks = near + far
    cot, first_edges = lax.optimization_barrier((cot, edges[0]))
    edges = (first_edges, edges[1])

    place = jnp.stack([y, zl])

    def local(kernel, shapes, operands, scratch):
        vmem = pl.BlockSpec(memory_space=pltpu.VMEM)
        return pl.pallas_call(
            kernel,
            out_shape=shapes,
            in_specs=[pl.BlockSpec(memory_space=pltpu.SMEM)] + [vmem] * len(operands),
            out_specs=jax.tree.map(lambda _: vmem, shapes),
            scratch_shapes=scratch,
            compiler_params=pltpu.CompilerParams(vmem_limit_bytes=48 * 1024 * 1024),
            cost_estimate=pl.CostEstimate(
                flops=10**8 * len(operands), bytes_accessed=3 * 10**6, transcendentals=0
            ),
        )(place, *operands)

    tiles = jax.ShapeDtypeStruct((64, 8, WIDTH), jnp.float32)
    rows = [pltpu.VMEM((STEPS, 6, DEPTH, 16, WIDTH), jnp.bfloat16)]
    grad, moved = local(
        gradient_kernel,
        (tiles, jax.ShapeDtypeStruct((2, 256, DEPTH * WIDTH), jnp.bfloat16)),
        (*blocks, cot),
        rows,
    )
    grad = local(edge_kernel, tiles, (*edges, moved, grad), [])
    weights, grad = lax.optimization_barrier((weights, grad))
    feat = local(
        forward_kernel,
        jax.ShapeDtypeStruct((16, ROWS, DEPTH, WIDTH), jnp.float32),
        (*blocks, *edges, weights),
        rows,
    )

    got = lax.all_to_all(grad, ("zl",) + SPACE, 0, 0, tiled=True)
    filter_grad = local(
        finish_kernel, jax.ShapeDtypeStruct((27, 8, 4), jnp.float32), (got,), []
    )

    rest = lax.ppermute(feat[8:], "zl", swap)
    kept = feat[:8]
    features_out = jnp.where(
        first,
        jnp.concatenate([kept, rest], axis=1),
        jnp.concatenate([rest, kept], axis=1),
    ) + bias_terms.astype(jnp.float32)[:, None, None, None]
    return (features_out, filter_grad)


def solution(mesh):
    fine = Mesh(mesh.devices.reshape(8, 2, 4, 4, 2), ("y", "zl", "x", "zh", "core"))
    filt = ("y", "zl")
    in_specs = (
        P(filt, SPACE, None, None),
        P(filt, SPACE, None, None),
        P(None, filt, None),
        P(filt),
    )
    out_specs = (P(filt, SPACE, None, None), P(None, filt, SPACE))
    return jax.shard_map(
        on_device, mesh=fine, in_specs=in_specs, out_specs=out_specs, check_vma=False
    )
```

```python
import math

import jax
import jax.numpy as jnp
from jax import lax
from jax.experimental import pallas as pl
from jax.experimental.pallas import tpu as pltpu
from jax.sharding import Mesh
from jax.sharding import PartitionSpec as P

SPACE = ("x", "zh", "core")
ROWS = 4
DEPTH = 8
WIDTH = 128
STEPS = 8
SCALE = 1.0 / math.sqrt(256 * DEPTH * WIDTH)


def fill(rows, place, blocks, edges):
    zl = place[1]
    for p, block in enumerate(blocks):
        rows[p, pl.ds(1 - zl, 5)] = block[...]
    rows[0:5, 5 * zl] = edges[0]
    rows[5:8, 5 * zl] = edges[1]


def cells_of(rows, row):
    return jnp.concatenate(
        [
            jnp.concatenate(
                [rows[p, row + dx, z] for dx in range(3) for p in range(STEPS)], axis=0
            )
            for z in range(DEPTH)
        ],
        axis=1,
    )


def forward_kernel(place, *refs):
    *blocks, near, far, weights, feat, rows = refs
    y = place[0]
    fill(rows, place, blocks, (near[...], far[...]))
    lane = lax.broadcasted_iota(jnp.int32, (16, WIDTH), 1)
    turned = pltpu.roll(
        weights[...].astype(jnp.float32).reshape(27 * 16, 128), lax.rem(128 - 16 * y + 32, 128), 1
    ).astype(jnp.bfloat16)
    taps = jnp.concatenate(
        [
            jnp.concatenate(
                [turned[16 * (9 * dx + q) : 16 * (9 * dx + q) + 16] for q in range(9)], axis=0
            )
            for dx in range(3)
        ],
        axis=1,
    )
    for row in range(ROWS):
        part = jnp.dot(taps, cells_of(rows, row), preferred_element_type=jnp.float32)
        for z in range(DEPTH):
            sums = []
            for dy in range(3):
                acc = None
                for dz in range(3):
                    if 0 <= z + dz - 1 < DEPTH:
                        at = 16 * (3 * dz + dy)
                        lo = WIDTH * (z + dz - 1)
                        term = part[at : at + 16, lo : lo + WIDTH]
                        acc = term if acc is None else acc + term
                sums.append(acc)
            left = jnp.where(lane == 0, 0.0, pltpu.roll(sums[0], 1, 1))
            right = jnp.where(lane == WIDTH - 1, 0.0, pltpu.roll(sums[2], WIDTH - 1, 1))
            feat[:, row, z, :] = sums[1] + left + right


def shifted(cot, row):
    lane = lax.broadcasted_iota(jnp.int32, (16, WIDTH), 1)
    gap = jnp.zeros((56, WIDTH), jnp.float32)
    empty = jnp.zeros((16, WIDTH), jnp.float32)
    moved = []
    for z in range(DEPTH):
        here = cot[row, z].astype(jnp.float32)
        ahead = jnp.where(lane == WIDTH - 1, 0.0, pltpu.roll(here, WIDTH - 1, 1))
        behind = jnp.where(lane == 0, 0.0, pltpu.roll(here, 1, 1))
        moved.append((ahead, here, behind))
    columns = []
    for z in range(DEPTH):
        column = []
        for half in range(2):
            for dz in range(3):
                for dy in range(3):
                    at = z - dz + 1
                    tile = moved[at][dy] if 0 <= at < DEPTH else empty
                    column.append(tile[8 * half : 8 * half + 8])
            column.append(gap)
        columns.append(jnp.concatenate(column, axis=0).astype(jnp.bfloat16))
    return jnp.concatenate(columns, axis=1)


def edge_cells(near, far):
    return jnp.concatenate(
        [
            jnp.concatenate(
                [near[p, z] for p in range(5)] + [far[p, z] for p in range(3)], axis=0
            )
            for z in range(DEPTH)
        ],
        axis=1,
    )


def over_cells(a, b):
    return lax.dot_general(a, b, (((1,), (1,)), ((), ())), preferred_element_type=jnp.float32)


def receivers(place, half):
    y, zl = place[0], place[1]
    base = 32 * lax.rem(zl + half, 2)
    return [base + lax.rem(y + k // 2 + 6, STEPS) * 4 + 2 * (k % 2) for k in range(16)]


def pair_of(one, two, k):
    sub = lax.broadcasted_iota(jnp.int32, (8, WIDTH), 0)
    a, b = one[8 * k : 8 * k + 8], two[8 * k : 8 * k + 8]
    return jnp.where(sub < 4, a, pltpu.roll(b, 4, 0)), jnp.where(sub < 4, pltpu.roll(a, 4, 0), b)


def gradient_kernel(place, *refs):
    *blocks, cot, grad, moved, rows = refs
    zeros = [jnp.zeros((count, DEPTH, 16, WIDTH), jnp.bfloat16) for count in (5, 3)]
    fill(rows, place, blocks, zeros)
    total = jnp.zeros((384, 256), jnp.float32)
    for row in range(ROWS):
        here = shifted(cot, row)
        if row in (0, 3):
            moved[row // 3] = here
        total = total + over_cells(cells_of(rows, row), here)
    wide = lax.broadcasted_iota(jnp.int32, (128, WIDTH), 1)
    for half in range(2):
        one, two, three = (
            total[128 * dx : 128 * dx + 128, WIDTH * half : WIDTH * half + WIDTH]
            for dx in range(3)
        )
        one = jnp.where(wide < 72, one, pltpu.roll(three, 72, 1))
        two = jnp.where(wide < 72, two, pltpu.roll(three, 32, 1))
        for k, at in enumerate(receivers(place, half)):
            grad[at], grad[at + 1] = pair_of(one, two, k)


def edge_kernel(place, near, far, moved, earlier, grad):
    zl = place[1]
    total = over_cells(edge_cells(near, far), moved[zl])
    wide = lax.broadcasted_iota(jnp.int32, (128, WIDTH), 1)
    low = zl == 0
    for half in range(2):
        part = total[:, WIDTH * half : WIDTH * half + WIDTH]
        one = jnp.where(low, part, jnp.where(wide < 72, 0.0, pltpu.roll(part, 72, 1)))
        two = jnp.where(
            jnp.logical_or(low, wide < 72), 0.0, pltpu.roll(part, 32, 1)
        )
        for k, at in enumerate(receivers(place, half)):
            first, second = pair_of(one, two, k)
            grad[at] = earlier[at] + first
            grad[at + 1] = earlier[at + 1] + second


def finish_kernel(place, got, out, turned, table):
    turned[...] = jnp.transpose(jnp.sum(got[...], axis=0) * SCALE)
    for o in range(8):
        for at, count, lane, start in ((0, 9, 0, 0), (9, 9, 4, 0), (18, 5, 0, 72), (23, 4, 4, 72)):
            part = turned[pl.ds(start + o, count, stride=8), :]
            table[at : at + count, 4 * o : 4 * o + 4] = part[:, lane : lane + 4]
    done = jnp.transpose(table[...])
    for o in range(8):
        out[o] = done[4 * o : 4 * o + 4, :27]


def on_device(activations, cotangent, filters, bias_terms):
    y, zl = lax.axis_index("y"), lax.axis_index("zl")
    acts = jnp.transpose(activations, (1, 2, 0, 3))
    cots = jnp.transpose(cotangent, (1, 2, 0, 3))
    first = zl == 0

    swap = [(0, 1), (1, 0)]
    other = lax.ppermute(lax.dynamic_slice_in_dim(acts, 3 * (1 - zl), 5, 0), "zl", swap)
    own = lax.dynamic_slice_in_dim(acts, 3 * zl, 5, 0)
    pairs = []
    for step in range(31):
        pairs += [(32 + step, step + 1), (step + 1, 32 + step)]

    mine = jnp.where(
        first,
        jnp.concatenate([own, other], axis=2),
        jnp.concatenate([other, own], axis=2),
    )
    give = jnp.concatenate(
        [lax.dynamic_slice_in_dim(cots, 4 * (1 - zl), 4, 0).reshape(32, 8, WIDTH), filters], axis=0
    )
    got = lax.ppermute(give, "zl", swap)

    def along(block, by):
        return lax.ppermute(block, "y", [(i, (i - by) % STEPS) for i in range(STEPS)])

    b2, b6 = along(mine, 2), along(mine, -2)
    keep = lax.dynamic_slice_in_dim(cots, 4 * zl, 4, 0)
    cot = jnp.concatenate([keep, got[:32].reshape(4, 8, 8, WIDTH)], axis=2)
    weights = jnp.concatenate([filters, got[32:]], axis=1)
    after, cot, weights = lax.optimization_barrier((mine, cot, weights))
    b1, b7 = along(after, 1), along(after, -1)
    turn = [
        ((2 * i + c), (2 * ((i + (2 if c else -2)) % STEPS) + c))
        for i in range(STEPS)
        for c in range(2)
    ]
    b4 = lax.ppermute(jnp.where(lax.axis_index("core") == 0, b2, b6), ("y", "core"), turn)
    b3, b5 = along(b2, 1), along(b6, -1)

    def outermost(blocks):
        return jnp.stack([jnp.where(first, block[0], block[4]) for block in blocks])

    near = (b6, b7, mine, b1, b2)
    send, b4 = lax.optimization_barrier((outermost(near), b4))
    far = (b3, b4, b5)
    edges = (
        lax.ppermute(send, ("zl",) + SPACE, pairs),
        lax.ppermute(outermost(far), ("zl",) + SPACE, pairs),
    )
    blocks = near + far
    cot, first_edges = lax.optimization_barrier((cot, edges[0]))
    edges = (first_edges, edges[1])

    place = jnp.stack([y, zl])

    def local(kernel, shapes, operands, scratch):
        vmem = pl.BlockSpec(memory_space=pltpu.VMEM)
        return pl.pallas_call(
            kernel,
            out_shape=shapes,
            in_specs=[pl.BlockSpec(memory_space=pltpu.SMEM)] + [vmem] * len(operands),
            out_specs=jax.tree.map(lambda _: vmem, shapes),
            scratch_shapes=scratch,
            compiler_params=pltpu.CompilerParams(vmem_limit_bytes=48 * 1024 * 1024),
            cost_estimate=pl.CostEstimate(
                flops=10**8 * len(operands), bytes_accessed=3 * 10**6, transcendentals=0
            ),
        )(place, *operands)

    tiles = jax.ShapeDtypeStruct((64, 8, WIDTH), jnp.float32)
    rows = [pltpu.VMEM((STEPS, 6, DEPTH, 16, WIDTH), jnp.bfloat16)]
    grad, moved = local(
        gradient_kernel,
        (tiles, jax.ShapeDtypeStruct((2, 256, DEPTH * WIDTH), jnp.bfloat16)),
        (*blocks, cot),
        rows,
    )
    grad = local(edge_kernel, tiles, (*edges, moved, grad), [])
    weights, grad = lax.optimization_barrier((weights, grad))
    feat = local(
        forward_kernel,
        jax.ShapeDtypeStruct((16, ROWS, DEPTH, WIDTH), jnp.float32),
        (*blocks, *edges, weights),
        rows,
    )

    got = lax.all_to_all(grad, ("zl",) + SPACE, 0, 0, tiled=True)
    filter_grad = local(
        finish_kernel,
        jax.ShapeDtypeStruct((8, 4, 27), jnp.float32),
        (got,),
        [pltpu.VMEM((WIDTH, 8), jnp.float32), pltpu.VMEM((32, WIDTH), jnp.float32)],
    ).transpose(2, 0, 1)

    rest = lax.ppermute(feat[8:], "zl", swap)
    kept = feat[:8]
    features_out = jnp.where(
        first,
        jnp.concatenate([kept, rest], axis=1),
        jnp.concatenate([rest, kept], axis=1),
    ) + bias_terms.astype(jnp.float32)[:, None, None, None]
    return (features_out, filter_grad)


def solution(mesh):
    fine = Mesh(mesh.devices.reshape(8, 2, 4, 4, 2), ("y", "zl", "x", "zh", "core"))
    filt = ("y", "zl")
    in_specs = (
        P(filt, SPACE, None, None),
        P(filt, SPACE, None, None),
        P(None, filt, None),
        P(filt),
    )
    out_specs = (P(filt, SPACE, None, None), P(None, filt, SPACE))
    return jax.shard_map(
        on_device, mesh=fine, in_specs=in_specs, out_specs=out_specs, check_vma=False
    )
```

```python
import math

import jax
import jax.numpy as jnp
from jax import lax
from jax.experimental import pallas as pl
from jax.experimental.pallas import tpu as pltpu
from jax.sharding import Mesh
from jax.sharding import PartitionSpec as P

SPACE = ("x", "zh", "core")
ROWS = 4
DEPTH = 8
WIDTH = 128
STEPS = 8
SCALE = 1.0 / math.sqrt(256 * DEPTH * WIDTH)


def fill(rows, place, blocks, edges):
    zl = place[1]
    for p, block in enumerate(blocks):
        rows[p, pl.ds(1 - zl, 5)] = block[...]
    rows[0:5, 5 * zl] = edges[0]
    rows[5:8, 5 * zl] = edges[1]


def cells_of(rows, row):
    return jnp.concatenate(
        [
            jnp.concatenate(
                [rows[p, row + dx, z] for dx in range(3) for p in range(STEPS)], axis=0
            )
            for z in range(DEPTH)
        ],
        axis=1,
    )


def forward_kernel(place, *refs):
    *blocks, near, far, weights, feat, rows = refs
    y = place[0]
    fill(rows, place, blocks, (near[...], far[...]))
    lane = lax.broadcasted_iota(jnp.int32, (16, WIDTH), 1)
    turned = pltpu.roll(
        weights[...].astype(jnp.float32).reshape(27 * 16, 128), lax.rem(128 - 16 * y + 32, 128), 1
    ).astype(jnp.bfloat16)
    taps = jnp.concatenate(
        [
            jnp.concatenate(
                [turned[16 * (9 * dx + q) : 16 * (9 * dx + q) + 16] for q in range(9)], axis=0
            )
            for dx in range(3)
        ],
        axis=1,
    )
    for row in range(ROWS):
        part = jnp.dot(taps, cells_of(rows, row), preferred_element_type=jnp.float32)
        for z in range(DEPTH):
            sums = []
            for dy in range(3):
                acc = None
                for dz in range(3):
                    if 0 <= z + dz - 1 < DEPTH:
                        at = 16 * (3 * dz + dy)
                        lo = WIDTH * (z + dz - 1)
                        term = part[at : at + 16, lo : lo + WIDTH]
                        acc = term if acc is None else acc + term
                sums.append(acc)
            left = jnp.where(lane == 0, 0.0, pltpu.roll(sums[0], 1, 1))
            right = jnp.where(lane == WIDTH - 1, 0.0, pltpu.roll(sums[2], WIDTH - 1, 1))
            feat[:, row, z, :] = sums[1] + left + right


def shifted(cot, row):
    lane = lax.broadcasted_iota(jnp.int32, (16, WIDTH), 1)
    gap = jnp.zeros((56, WIDTH), jnp.float32)
    empty = jnp.zeros((16, WIDTH), jnp.float32)
    moved = []
    for z in range(DEPTH):
        here = cot[row, z].astype(jnp.float32)
        ahead = jnp.where(lane == WIDTH - 1, 0.0, pltpu.roll(here, WIDTH - 1, 1))
        behind = jnp.where(lane == 0, 0.0, pltpu.roll(here, 1, 1))
        moved.append((ahead, here, behind))
    columns = []
    for z in range(DEPTH):
        column = []
        for half in range(2):
            for dz in range(3):
                for dy in range(3):
                    at = z - dz + 1
                    tile = moved[at][dy] if 0 <= at < DEPTH else empty
                    column.append(tile[8 * half : 8 * half + 8])
            column.append(gap)
        columns.append(jnp.concatenate(column, axis=0).astype(jnp.bfloat16))
    return jnp.concatenate(columns, axis=1)


def over_cells(a, b):
    return lax.dot_general(a, b, (((1,), (1,)), ((), ())), preferred_element_type=jnp.float32)


def receivers(place, half, p):
    y, zl = place[0], place[1]
    return 32 * lax.rem(zl + half, 2) + 4 * lax.rem(y + p + 6, STEPS)


def pair_of(one, two, k):
    sub = lax.broadcasted_iota(jnp.int32, (8, WIDTH), 0)
    a, b = one[8 * k : 8 * k + 8], two[8 * k : 8 * k + 8]
    return jnp.where(sub < 4, a, pltpu.roll(b, 4, 0)), jnp.where(sub < 4, pltpu.roll(a, 4, 0), b)


def gradient_kernel(place, *refs):
    *blocks, edge, cot, grad, later, moved, rows, tiles, sems = refs
    fill(rows, place, blocks, (edge[...], jnp.zeros((3, DEPTH, 16, WIDTH), jnp.bfloat16)))
    total = jnp.zeros((384, 256), jnp.float32)
    for row in range(ROWS):
        here = shifted(cot, row)
        if row in (0, 3):
            moved[row // 3] = here
        total = total + over_cells(cells_of(rows, row), here)
    wide = lax.broadcasted_iota(jnp.int32, (128, WIDTH), 1)
    copies = []
    for half in range(2):
        one, two, three = (
            total[128 * dx : 128 * dx + 128, WIDTH * half : WIDTH * half + WIDTH]
            for dx in range(3)
        )
        one = jnp.where(wide < 72, one, pltpu.roll(three, 72, 1))
        two = jnp.where(wide < 72, two, pltpu.roll(three, 32, 1))
        for p in range(STEPS):
            n = 5 * half + p
            into = tiles.at[n] if p < 5 else later.at[3 * half + p - 5]
            into[0], into[1] = pair_of(one, two, 2 * p)
            into[2], into[3] = pair_of(one, two, 2 * p + 1)
            if p < 5:
                at = receivers(place, half, p)
                copies.append(pltpu.make_async_copy(into, grad.at[pl.ds(at, 4)], sems.at[n]))
                copies[-1].start()
    for copy in copies:
        copy.wait()


def edge_kernel(place, edge, moved, earlier, _, grad, tiles, sems):
    zl = place[1]
    cells = jnp.concatenate(
        [jnp.concatenate([edge[p, z] for p in range(3)], axis=0) for z in range(DEPTH)], axis=1
    )
    total = over_cells(cells, moved[zl])
    wide = lax.broadcasted_iota(jnp.int32, (48, WIDTH), 1)
    low = zl == 0
    copies = []
    for half in range(2):
        part = total[:, WIDTH * half : WIDTH * half + WIDTH]
        one = jnp.where(low, part, jnp.where(wide < 72, 0.0, pltpu.roll(part, 72, 1)))
        two = jnp.where(jnp.logical_or(low, wide < 72), 0.0, pltpu.roll(part, 32, 1))
        for p in range(3):
            n = 3 * half + p
            for k in range(2):
                first, second = pair_of(one, two, 2 * p + k)
                tiles[n, 2 * k] = earlier[n, 2 * k] + first
                tiles[n, 2 * k + 1] = earlier[n, 2 * k + 1] + second
            at = receivers(place, half, p + 5)
            copies.append(pltpu.make_async_copy(tiles.at[n], grad.at[pl.ds(at, 4)], sems.at[n]))
            copies[-1].start()
    for copy in copies:
        copy.wait()


def finish_kernel(place, got, out, turned, table):
    turned[...] = jnp.transpose(jnp.sum(got[...], axis=0) * SCALE)
    for o in range(8):
        for at, count, lane, start in ((0, 9, 0, 0), (9, 9, 4, 0), (18, 5, 0, 72), (23, 4, 4, 72)):
            part = turned[pl.ds(start + o, count, stride=8), :]
            table[at : at + count, 4 * o : 4 * o + 4] = part[:, lane : lane + 4]
    done = jnp.transpose(table[...])
    for o in range(8):
        out[o] = done[4 * o : 4 * o + 4, :27]


def on_device(activations, cotangent, filters, bias_terms):
    y, zl = lax.axis_index("y"), lax.axis_index("zl")
    acts = jnp.transpose(activations, (1, 2, 0, 3))
    cots = jnp.transpose(cotangent, (1, 2, 0, 3))
    first = zl == 0

    swap = [(0, 1), (1, 0)]
    other = lax.ppermute(
        lax.dynamic_slice_in_dim(activations, 3 * (1 - zl), 5, 1), "zl", swap
    ).transpose(1, 2, 0, 3)
    own = lax.dynamic_slice_in_dim(acts, 3 * zl, 5, 0)
    pairs = []
    for step in range(31):
        pairs += [(32 + step, step + 1), (step + 1, 32 + step)]

    mine = jnp.where(
        first,
        jnp.concatenate([own, other], axis=2),
        jnp.concatenate([other, own], axis=2),
    )
    give = jnp.concatenate(
        [lax.dynamic_slice_in_dim(cots, 4 * (1 - zl), 4, 0).reshape(32, 8, WIDTH), filters], axis=0
    )
    got = lax.ppermute(give, "zl", swap)

    def along(block, by):
        return lax.ppermute(block, "y", [(i, (i - by) % STEPS) for i in range(STEPS)])

    b2, b6 = along(mine, 2), along(mine, -2)
    keep = lax.dynamic_slice_in_dim(cots, 4 * zl, 4, 0)
    cot = jnp.concatenate([keep, got[:32].reshape(4, 8, 8, WIDTH)], axis=2)
    weights = jnp.concatenate([filters, got[32:]], axis=1)
    after, cot, weights = lax.optimization_barrier((mine, cot, weights))
    b1, b7 = along(after, 1), along(after, -1)
    turn = [
        ((2 * i + c), (2 * ((i + (2 if c else -2)) % STEPS) + c))
        for i in range(STEPS)
        for c in range(2)
    ]
    b4 = lax.ppermute(jnp.where(lax.axis_index("core") == 0, b2, b6), ("y", "core"), turn)
    b3, b5 = along(b2, 1), along(b6, -1)

    def outermost(blocks):
        return jnp.stack([jnp.where(first, block[0], block[4]) for block in blocks])

    near = (b6, b7, mine, b1, b2)
    send, b4 = lax.optimization_barrier((outermost(near), b4))
    far = (b3, b4, b5)
    edges = (
        lax.ppermute(send, ("zl",) + SPACE, pairs),
        lax.ppermute(outermost(far), ("zl",) + SPACE, pairs),
    )
    blocks = near + far
    place = jnp.stack([y, zl])

    vmem, hbm = (pl.BlockSpec(memory_space=space) for space in (pltpu.VMEM, pltpu.HBM))

    def local(kernel, shapes, operands, scratch, out_specs=vmem, alias=False):
        return pl.pallas_call(
            kernel,
            out_shape=shapes,
            in_specs=[pl.BlockSpec(memory_space=pltpu.SMEM)]
            + [vmem] * (len(operands) - alias)
            + [hbm] * alias,
            out_specs=out_specs,
            scratch_shapes=scratch,
            input_output_aliases={len(operands): 0} if alias else {},
            compiler_params=pltpu.CompilerParams(vmem_limit_bytes=48 * 1024 * 1024),
            cost_estimate=pl.CostEstimate(
                flops=10**8 * len(operands), bytes_accessed=3 * 10**6, transcendentals=0
            ),
        )(place, *operands)

    def tiles_of(*counts):
        return jax.ShapeDtypeStruct((*counts, 8, WIDTH), jnp.float32)

    rows = [pltpu.VMEM((STEPS, 6, DEPTH, 16, WIDTH), jnp.bfloat16)]
    grad, later, moved = local(
        gradient_kernel,
        (
            tiles_of(64),
            tiles_of(6, 4),
            jax.ShapeDtypeStruct((2, 256, DEPTH * WIDTH), jnp.bfloat16),
        ),
        (*blocks, edges[0], cot),
        rows + [pltpu.VMEM((10, 4, 8, WIDTH), jnp.float32), pltpu.SemaphoreType.DMA((10,))],
        (hbm, vmem, vmem),
    )
    grad = local(
        edge_kernel,
        tiles_of(64),
        (edges[1], moved, later, grad),
        [pltpu.VMEM((6, 4, 8, WIDTH), jnp.float32), pltpu.SemaphoreType.DMA((6,))],
        hbm,
        True,
    )
    weights, grad = lax.optimization_barrier((weights, grad))
    feat = local(
        forward_kernel,
        jax.ShapeDtypeStruct((16, ROWS, DEPTH, WIDTH), jnp.float32),
        (*blocks, *edges, weights),
        rows,
    )

    got = lax.all_to_all(grad, ("zl",) + SPACE, 0, 0, tiled=True)
    filter_grad = local(
        finish_kernel,
        jax.ShapeDtypeStruct((8, 4, 27), jnp.float32),
        (got,),
        [pltpu.VMEM((WIDTH, 8), jnp.float32), pltpu.VMEM((32, WIDTH), jnp.float32)],
    ).transpose(2, 0, 1)

    rest = lax.ppermute(feat[8:], "zl", swap)
    kept = feat[:8]
    features_out = jnp.where(
        first,
        jnp.concatenate([kept, rest], axis=1),
        jnp.concatenate([rest, kept], axis=1),
    ) + bias_terms.astype(jnp.float32)[:, None, None, None]
    return (features_out, filter_grad)


def solution(mesh):
    fine = Mesh(mesh.devices.reshape(8, 2, 4, 4, 2), ("y", "zl", "x", "zh", "core"))
    filt = ("y", "zl")
    in_specs = (
        P(filt, SPACE, None, None),
        P(filt, SPACE, None, None),
        P(None, filt, None),
        P(filt),
    )
    out_specs = (P(filt, SPACE, None, None), P(None, filt, SPACE))
    return jax.shard_map(
        on_device, mesh=fine, in_specs=in_specs, out_specs=out_specs, check_vma=False
    )
```

```python
import math

import jax
import jax.numpy as jnp
from jax import lax
from jax.experimental import pallas as pl
from jax.experimental.pallas import tpu as pltpu
from jax.sharding import Mesh
from jax.sharding import PartitionSpec as P

SPACE = ("x", "zh", "core")
ROWS = 4
DEPTH = 8
WIDTH = 128
STEPS = 8
SCALE = 1.0 / math.sqrt(256 * DEPTH * WIDTH)


def fill(rows, place, blocks, edges):
    zl = place[1]
    for p, block in enumerate(blocks):
        rows[p, pl.ds(1 - zl, 5)] = block[...]
    rows[0:5, 5 * zl] = edges[0]
    rows[5:8, 5 * zl] = edges[1]


def cells_of(rows, row):
    return jnp.concatenate(
        [
            jnp.concatenate(
                [rows[p, row + dx, z] for dx in range(3) for p in range(STEPS)], axis=0
            )
            for z in range(DEPTH)
        ],
        axis=1,
    )


def forward_kernel(place, *refs):
    *blocks, near, far, weights, feat, rows = refs
    y = place[0]
    fill(rows, place, blocks, (near[...], far[...]))
    lane = lax.broadcasted_iota(jnp.int32, (16, WIDTH), 1)
    turned = pltpu.roll(
        weights[...].astype(jnp.float32).reshape(27 * 16, 128), lax.rem(128 - 16 * y + 32, 128), 1
    ).astype(jnp.bfloat16)
    taps = jnp.concatenate(
        [
            jnp.concatenate(
                [turned[16 * (9 * dx + q) : 16 * (9 * dx + q) + 16] for q in range(9)], axis=0
            )
            for dx in range(3)
        ],
        axis=1,
    )
    for row in range(ROWS):
        part = jnp.dot(taps, cells_of(rows, row), preferred_element_type=jnp.float32)
        for z in range(DEPTH):
            sums = []
            for dy in range(3):
                acc = None
                for dz in range(3):
                    if 0 <= z + dz - 1 < DEPTH:
                        at = 16 * (3 * dz + dy)
                        lo = WIDTH * (z + dz - 1)
                        term = part[at : at + 16, lo : lo + WIDTH]
                        acc = term if acc is None else acc + term
                sums.append(acc)
            left = jnp.where(lane == 0, 0.0, pltpu.roll(sums[0], 1, 1))
            right = jnp.where(lane == WIDTH - 1, 0.0, pltpu.roll(sums[2], WIDTH - 1, 1))
            feat[:, row, z, :] = sums[1] + left + right


def shifted(cot, row):
    lane = lax.broadcasted_iota(jnp.int32, (16, WIDTH), 1)
    gap = jnp.zeros((56, WIDTH), jnp.float32)
    empty = jnp.zeros((16, WIDTH), jnp.float32)
    moved = []
    for z in range(DEPTH):
        here = cot[row, z].astype(jnp.float32)
        ahead = jnp.where(lane == WIDTH - 1, 0.0, pltpu.roll(here, WIDTH - 1, 1))
        behind = jnp.where(lane == 0, 0.0, pltpu.roll(here, 1, 1))
        moved.append((ahead, here, behind))
    columns = []
    for z in range(DEPTH):
        column = []
        for half in range(2):
            for dz in range(3):
                for dy in range(3):
                    at = z - dz + 1
                    tile = moved[at][dy] if 0 <= at < DEPTH else empty
                    column.append(tile[8 * half : 8 * half + 8])
            column.append(gap)
        columns.append(jnp.concatenate(column, axis=0).astype(jnp.bfloat16))
    return jnp.concatenate(columns, axis=1)


def edge_cells(near, far):
    return jnp.concatenate(
        [
            jnp.concatenate(
                [near[p, z] for p in range(5)] + [far[p, z] for p in range(3)], axis=0
            )
            for z in range(DEPTH)
        ],
        axis=1,
    )


def over_cells(a, b):
    return lax.dot_general(a, b, (((1,), (1,)), ((), ())), preferred_element_type=jnp.float32)


def receivers(place, half):
    y, zl = place[0], place[1]
    base = 32 * lax.rem(zl + half, 2)
    return [base + lax.rem(y + k // 2 + 6, STEPS) * 4 + 2 * (k % 2) for k in range(16)]


def pair_of(one, two, k):
    sub = lax.broadcasted_iota(jnp.int32, (8, WIDTH), 0)
    a, b = one[8 * k : 8 * k + 8], two[8 * k : 8 * k + 8]
    return jnp.where(sub < 4, a, pltpu.roll(b, 4, 0)), jnp.where(sub < 4, pltpu.roll(a, 4, 0), b)


def gradient_kernel(place, *refs):
    *blocks, cot, grad, moved, rows = refs
    zeros = [jnp.zeros((count, DEPTH, 16, WIDTH), jnp.bfloat16) for count in (5, 3)]
    fill(rows, place, blocks, zeros)
    total = jnp.zeros((384, 256), jnp.float32)
    for row in range(ROWS):
        here = shifted(cot, row)
        if row in (0, 3):
            moved[row // 3] = here
        total = total + over_cells(cells_of(rows, row), here)
    wide = lax.broadcasted_iota(jnp.int32, (128, WIDTH), 1)
    for half in range(2):
        one, two, three = (
            total[128 * dx : 128 * dx + 128, WIDTH * half : WIDTH * half + WIDTH]
            for dx in range(3)
        )
        one = jnp.where(wide < 72, one, pltpu.roll(three, 72, 1))
        two = jnp.where(wide < 72, two, pltpu.roll(three, 32, 1))
        for k, at in enumerate(receivers(place, half)):
            grad[at], grad[at + 1] = pair_of(one, two, k)


def edge_kernel(place, near, far, moved, earlier, grad):
    zl = place[1]
    total = over_cells(edge_cells(near, far), moved[zl])
    wide = lax.broadcasted_iota(jnp.int32, (128, WIDTH), 1)
    low = zl == 0
    for half in range(2):
        part = total[:, WIDTH * half : WIDTH * half + WIDTH]
        one = jnp.where(low, part, jnp.where(wide < 72, 0.0, pltpu.roll(part, 72, 1)))
        two = jnp.where(
            jnp.logical_or(low, wide < 72), 0.0, pltpu.roll(part, 32, 1)
        )
        for k, at in enumerate(receivers(place, half)):
            first, second = pair_of(one, two, k)
            grad[at] = earlier[at] + first
            grad[at + 1] = earlier[at + 1] + second


def finish_kernel(place, got, out, turned, table):
    turned[...] = jnp.transpose(jnp.sum(got[...], axis=0) * SCALE)
    for o in range(8):
        for at, count, lane, start in ((0, 9, 0, 0), (9, 9, 4, 0), (18, 5, 0, 72), (23, 4, 4, 72)):
            part = turned[pl.ds(start + o, count, stride=8), :]
            table[at : at + count, 4 * o : 4 * o + 4] = part[:, lane : lane + 4]
    done = jnp.transpose(table[...])
    for o in range(8):
        out[o] = done[4 * o : 4 * o + 4, :27]


def on_device(activations, cotangent, filters, bias_terms):
    y, zl = lax.axis_index("y"), lax.axis_index("zl")
    acts = jnp.transpose(activations, (1, 2, 0, 3))
    cots = jnp.transpose(cotangent, (1, 2, 0, 3))
    first = zl == 0

    swap = [(0, 1), (1, 0)]
    other = lax.ppermute(lax.dynamic_slice_in_dim(acts, 3 * (1 - zl), 5, 0), "zl", swap)
    own = lax.dynamic_slice_in_dim(acts, 3 * zl, 5, 0)
    pairs = []
    for step in range(31):
        pairs += [(32 + step, step + 1), (step + 1, 32 + step)]

    mine = jnp.where(
        first,
        jnp.concatenate([own, other], axis=2),
        jnp.concatenate([other, own], axis=2),
    )
    give = jnp.concatenate(
        [lax.dynamic_slice_in_dim(cots, 4 * (1 - zl), 4, 0).reshape(32, 8, WIDTH), filters], axis=0
    )
    got = lax.ppermute(give, "zl", swap)

    def along(block, by):
        return lax.ppermute(block, "y", [(i, (i - by) % STEPS) for i in range(STEPS)])

    b1, b7 = along(mine, 1), along(mine, -1)
    keep = lax.dynamic_slice_in_dim(cots, 4 * zl, 4, 0)
    cot = jnp.concatenate([keep, got[:32].reshape(4, 8, 8, WIDTH)], axis=2)
    weights = jnp.concatenate([filters, got[32:]], axis=1)
    b7, cot, weights = lax.optimization_barrier((b7, cot, weights))
    b2, b6 = along(b1, 1), along(b7, -1)
    turn = [
        ((2 * i + c), (2 * ((i + (2 if c else -2)) % STEPS) + c))
        for i in range(STEPS)
        for c in range(2)
    ]
    b4 = lax.ppermute(jnp.where(lax.axis_index("core") == 0, b2, b6), ("y", "core"), turn)
    b3, b5 = along(b2, 1), along(b6, -1)

    def outermost(blocks):
        return jnp.stack([jnp.where(first, block[0], block[4]) for block in blocks])

    near = (b6, b7, mine, b1, b2)
    send, b4 = lax.optimization_barrier((outermost(near), b4))
    far = (b3, b4, b5)
    edges = (
        lax.ppermute(send, ("zl",) + SPACE, pairs),
        lax.ppermute(outermost(far), ("zl",) + SPACE, pairs),
    )
    blocks = near + far
    cot, first_edges = lax.optimization_barrier((cot, edges[0]))
    edges = (first_edges, edges[1])

    place = jnp.stack([y, zl])

    def local(kernel, shapes, operands, scratch):
        vmem = pl.BlockSpec(memory_space=pltpu.VMEM)
        return pl.pallas_call(
            kernel,
            out_shape=shapes,
            in_specs=[pl.BlockSpec(memory_space=pltpu.SMEM)] + [vmem] * len(operands),
            out_specs=jax.tree.map(lambda _: vmem, shapes),
            scratch_shapes=scratch,
            compiler_params=pltpu.CompilerParams(vmem_limit_bytes=48 * 1024 * 1024),
            cost_estimate=pl.CostEstimate(
                flops=10**8 * len(operands), bytes_accessed=3 * 10**6, transcendentals=0
            ),
        )(place, *operands)

    tiles = jax.ShapeDtypeStruct((64, 8, WIDTH), jnp.float32)
    rows = [pltpu.VMEM((STEPS, 6, DEPTH, 16, WIDTH), jnp.bfloat16)]
    grad, moved = local(
        gradient_kernel,
        (tiles, jax.ShapeDtypeStruct((2, 256, DEPTH * WIDTH), jnp.bfloat16)),
        (*blocks, cot),
        rows,
    )
    grad = local(edge_kernel, tiles, (*edges, moved, grad), [])
    weights, grad = lax.optimization_barrier((weights, grad))
    feat = local(
        forward_kernel,
        jax.ShapeDtypeStruct((16, ROWS, DEPTH, WIDTH), jnp.float32),
        (*blocks, *edges, weights),
        rows,
    )

    got = lax.all_to_all(grad, ("zl",) + SPACE, 0, 0, tiled=True)
    filter_grad = local(
        finish_kernel,
        jax.ShapeDtypeStruct((8, 4, 27), jnp.float32),
        (got,),
        [pltpu.VMEM((WIDTH, 8), jnp.float32), pltpu.VMEM((32, WIDTH), jnp.float32)],
    ).transpose(2, 0, 1)

    rest = lax.ppermute(feat[8:], "zl", swap)
    kept = feat[:8]
    features_out = jnp.where(
        first,
        jnp.concatenate([kept, rest], axis=1),
        jnp.concatenate([rest, kept], axis=1),
    ) + bias_terms.astype(jnp.float32)[:, None, None, None]
    return (features_out, filter_grad)


def solution(mesh):
    fine = Mesh(mesh.devices.reshape(8, 2, 4, 4, 2), ("y", "zl", "x", "zh", "core"))
    filt = ("y", "zl")
    in_specs = (
        P(filt, SPACE, None, None),
        P(filt, SPACE, None, None),
        P(None, filt, None),
        P(filt),
    )
    out_specs = (P(filt, SPACE, None, None), P(None, filt, SPACE))
    return jax.shard_map(
        on_device, mesh=fine, in_specs=in_specs, out_specs=out_specs, check_vma=False
    )
```

```python
import math

import jax
import jax.numpy as jnp
from jax import lax
from jax.experimental import pallas as pl
from jax.experimental.pallas import tpu as pltpu
from jax.sharding import Mesh
from jax.sharding import PartitionSpec as P

SPACE = ("x", "zh", "core")
ROWS = 4
DEPTH = 8
WIDTH = 128
STEPS = 8
SCALE = 1.0 / math.sqrt(256 * DEPTH * WIDTH)


def fill(rows, place, blocks, edges):
    zl = place[1]
    for p, block in enumerate(blocks):
        rows[p, pl.ds(1 - zl, 5)] = block[...]
    rows[0:5, 5 * zl] = edges[0]
    rows[5:8, 5 * zl] = edges[1]


def cells_of(rows, row):
    return jnp.concatenate(
        [
            jnp.concatenate(
                [rows[p, row + dx, z] for dx in range(3) for p in range(STEPS)], axis=0
            )
            for z in range(DEPTH)
        ],
        axis=1,
    )


def forward_kernel(place, *refs):
    *blocks, near, far, weights, feat, rows = refs
    y = place[0]
    fill(rows, place, blocks, (near[...], far[...]))
    lane = lax.broadcasted_iota(jnp.int32, (16, WIDTH), 1)
    turned = pltpu.roll(
        weights[...].astype(jnp.float32).reshape(27 * 16, 128), lax.rem(128 - 16 * y + 32, 128), 1
    ).astype(jnp.bfloat16)
    taps = jnp.concatenate(
        [
            jnp.concatenate(
                [turned[16 * (9 * dx + q) : 16 * (9 * dx + q) + 16] for q in range(9)], axis=0
            )
            for dx in range(3)
        ],
        axis=1,
    )
    for row in range(ROWS):
        part = jnp.dot(taps, cells_of(rows, row), preferred_element_type=jnp.float32)
        for z in range(DEPTH):
            sums = []
            for dy in range(3):
                acc = None
                for dz in range(3):
                    if 0 <= z + dz - 1 < DEPTH:
                        at = 16 * (3 * dz + dy)
                        lo = WIDTH * (z + dz - 1)
                        term = part[at : at + 16, lo : lo + WIDTH]
                        acc = term if acc is None else acc + term
                sums.append(acc)
            left = jnp.where(lane == 0, 0.0, pltpu.roll(sums[0], 1, 1))
            right = jnp.where(lane == WIDTH - 1, 0.0, pltpu.roll(sums[2], WIDTH - 1, 1))
            feat[:, row, z, :] = sums[1] + left + right


def shifted(cot, row):
    lane = lax.broadcasted_iota(jnp.int32, (16, WIDTH), 1)
    gap = jnp.zeros((56, WIDTH), jnp.float32)
    empty = jnp.zeros((16, WIDTH), jnp.float32)
    moved = []
    for z in range(DEPTH):
        here = cot[row, z].astype(jnp.float32)
        ahead = jnp.where(lane == WIDTH - 1, 0.0, pltpu.roll(here, WIDTH - 1, 1))
        behind = jnp.where(lane == 0, 0.0, pltpu.roll(here, 1, 1))
        moved.append((ahead, here, behind))
    columns = []
    for z in range(DEPTH):
        column = []
        for half in range(2):
            for dz in range(3):
                for dy in range(3):
                    at = z - dz + 1
                    tile = moved[at][dy] if 0 <= at < DEPTH else empty
                    column.append(tile[8 * half : 8 * half + 8])
            column.append(gap)
        columns.append(jnp.concatenate(column, axis=0).astype(jnp.bfloat16))
    return jnp.concatenate(columns, axis=1)


def edge_cells(near, far):
    return jnp.concatenate(
        [
            jnp.concatenate(
                [near[p, z] for p in range(5)] + [far[p, z] for p in range(3)], axis=0
            )
            for z in range(DEPTH)
        ],
        axis=1,
    )


def over_cells(a, b):
    return lax.dot_general(a, b, (((1,), (1,)), ((), ())), preferred_element_type=jnp.float32)


def receivers(place, half):
    y, zl = place[0], place[1]
    base = 32 * lax.rem(zl + half, 2)
    return [base + lax.rem(y + k // 2 + 6, STEPS) * 4 + 2 * (k % 2) for k in range(16)]


def pair_of(one, two, k):
    sub = lax.broadcasted_iota(jnp.int32, (8, WIDTH), 0)
    a, b = one[8 * k : 8 * k + 8], two[8 * k : 8 * k + 8]
    return jnp.where(sub < 4, a, pltpu.roll(b, 4, 0)), jnp.where(sub < 4, pltpu.roll(a, 4, 0), b)


def gradient_kernel(place, *refs):
    *blocks, cot, grad, moved, rows = refs
    zeros = [jnp.zeros((count, DEPTH, 16, WIDTH), jnp.bfloat16) for count in (5, 3)]
    fill(rows, place, blocks, zeros)
    total = jnp.zeros((384, 256), jnp.float32)
    for row in range(ROWS):
        here = shifted(cot, row)
        if row in (0, 3):
            moved[row // 3] = here
        total = total + over_cells(cells_of(rows, row), here)
    wide = lax.broadcasted_iota(jnp.int32, (128, WIDTH), 1)
    for half in range(2):
        one, two, three = (
            total[128 * dx : 128 * dx + 128, WIDTH * half : WIDTH * half + WIDTH]
            for dx in range(3)
        )
        one = jnp.where(wide < 72, one, pltpu.roll(three, 72, 1))
        two = jnp.where(wide < 72, two, pltpu.roll(three, 32, 1))
        for k, at in enumerate(receivers(place, half)):
            grad[at], grad[at + 1] = pair_of(one, two, k)


def edge_kernel(place, near, far, moved, earlier, grad):
    zl = place[1]
    total = over_cells(edge_cells(near, far), moved[zl])
    wide = lax.broadcasted_iota(jnp.int32, (128, WIDTH), 1)
    low = zl == 0
    for half in range(2):
        part = total[:, WIDTH * half : WIDTH * half + WIDTH]
        one = jnp.where(low, part, jnp.where(wide < 72, 0.0, pltpu.roll(part, 72, 1)))
        two = jnp.where(
            jnp.logical_or(low, wide < 72), 0.0, pltpu.roll(part, 32, 1)
        )
        for k, at in enumerate(receivers(place, half)):
            first, second = pair_of(one, two, k)
            grad[at] = earlier[at] + first
            grad[at + 1] = earlier[at + 1] + second


def finish_kernel(place, got, out, turned, table):
    turned[...] = jnp.transpose(jnp.sum(got[...], axis=0) * SCALE)
    for o in range(8):
        for at, count, lane, start in ((0, 9, 0, 0), (9, 9, 4, 0), (18, 5, 0, 72), (23, 4, 4, 72)):
            part = turned[pl.ds(start + o, count, stride=8), :]
            table[at : at + count, 4 * o : 4 * o + 4] = part[:, lane : lane + 4]
    done = jnp.transpose(table[...])
    for o in range(8):
        out[o] = done[4 * o : 4 * o + 4, :27]


def on_device(activations, cotangent, filters, bias_terms):
    y, zl = lax.axis_index("y"), lax.axis_index("zl")
    acts = jnp.transpose(activations, (1, 2, 0, 3))
    cots = jnp.transpose(cotangent, (1, 2, 0, 3))
    first = zl == 0

    swap = [(0, 1), (1, 0)]
    other = lax.ppermute(lax.dynamic_slice_in_dim(acts, 3 * (1 - zl), 5, 0), "zl", swap)
    own = lax.dynamic_slice_in_dim(acts, 3 * zl, 5, 0)
    pairs = []
    for step in range(31):
        pairs += [(32 + step, step + 1), (step + 1, 32 + step)]

    mine = jnp.where(
        first,
        jnp.concatenate([own, other], axis=2),
        jnp.concatenate([other, own], axis=2),
    )
    got = lax.ppermute(lax.dynamic_slice_in_dim(cots, 4 * (1 - zl), 4, 0), "zl", swap)

    def along(block, by):
        return lax.ppermute(block, "y", [(i, (i - by) % STEPS) for i in range(STEPS)])

    b2, b6 = along(mine, 2), along(mine, -2)
    keep = lax.dynamic_slice_in_dim(cots, 4 * zl, 4, 0)
    cot = jnp.concatenate([keep, got], axis=2)
    after, cot = lax.optimization_barrier((mine, cot))
    b1, b7 = along(after, 1), along(after, -1)
    turn = [
        ((2 * i + c), (2 * ((i + (2 if c else -2)) % STEPS) + c))
        for i in range(STEPS)
        for c in range(2)
    ]
    b4 = lax.ppermute(jnp.where(lax.axis_index("core") == 0, b2, b6), ("y", "core"), turn)
    b3, b5 = along(b2, 1), along(b6, -1)

    def outermost(blocks):
        return jnp.stack([jnp.where(first, block[0], block[4]) for block in blocks])

    near = (b6, b7, mine, b1, b2)
    send, b4 = lax.optimization_barrier((outermost(near), b4))
    far = (b3, b4, b5)
    carried = jnp.pad(filters.reshape(216, WIDTH), ((0, 8), (0, 0))).reshape(14, 16, WIDTH)
    carried = jnp.concatenate([send.reshape(40, 16, WIDTH), carried], axis=0)
    carried = lax.ppermute(carried, ("zl",) + SPACE, pairs + [(63, 0), (0, 63)])
    cot, carried = lax.optimization_barrier((cot, carried))
    space = lax.axis_index(SPACE)
    at_end = jnp.where(first, space == 0, space == 31)
    edges = (
        jnp.where(at_end, 0, carried[:40]).reshape(5, DEPTH, 16, WIDTH),
        lax.ppermute(outermost(far), ("zl",) + SPACE, pairs),
    )
    theirs = carried[40:].reshape(224, WIDTH)[:216].reshape(27, 8, WIDTH)
    weights = jnp.concatenate([filters, theirs], axis=1)
    blocks = near + far

    place = jnp.stack([y, zl])

    def local(kernel, shapes, operands, scratch):
        vmem = pl.BlockSpec(memory_space=pltpu.VMEM)
        return pl.pallas_call(
            kernel,
            out_shape=shapes,
            in_specs=[pl.BlockSpec(memory_space=pltpu.SMEM)] + [vmem] * len(operands),
            out_specs=jax.tree.map(lambda _: vmem, shapes),
            scratch_shapes=scratch,
            compiler_params=pltpu.CompilerParams(vmem_limit_bytes=48 * 1024 * 1024),
            cost_estimate=pl.CostEstimate(
                flops=10**8 * len(operands), bytes_accessed=3 * 10**6, transcendentals=0
            ),
        )(place, *operands)

    tiles = jax.ShapeDtypeStruct((64, 8, WIDTH), jnp.float32)
    rows = [pltpu.VMEM((STEPS, 6, DEPTH, 16, WIDTH), jnp.bfloat16)]
    grad, moved = local(
        gradient_kernel,
        (tiles, jax.ShapeDtypeStruct((2, 256, DEPTH * WIDTH), jnp.bfloat16)),
        (*blocks, cot),
        rows,
    )
    grad = local(edge_kernel, tiles, (*edges, moved, grad), [])
    weights, grad = lax.optimization_barrier((weights, grad))
    feat = local(
        forward_kernel,
        jax.ShapeDtypeStruct((16, ROWS, DEPTH, WIDTH), jnp.float32),
        (*blocks, *edges, weights),
        rows,
    )

    got = lax.all_to_all(grad, ("zl",) + SPACE, 0, 0, tiled=True)
    filter_grad = local(
        finish_kernel,
        jax.ShapeDtypeStruct((8, 4, 27), jnp.float32),
        (got,),
        [pltpu.VMEM((WIDTH, 8), jnp.float32), pltpu.VMEM((32, WIDTH), jnp.float32)],
    ).transpose(2, 0, 1)

    rest = lax.ppermute(feat[8:], "zl", swap)
    kept = feat[:8]
    features_out = jnp.where(
        first,
        jnp.concatenate([kept, rest], axis=1),
        jnp.concatenate([rest, kept], axis=1),
    ) + bias_terms.astype(jnp.float32)[:, None, None, None]
    return (features_out, filter_grad)


def solution(mesh):
    fine = Mesh(mesh.devices.reshape(8, 2, 4, 4, 2), ("y", "zl", "x", "zh", "core"))
    filt = ("y", "zl")
    in_specs = (
        P(filt, SPACE, None, None),
        P(filt, SPACE, None, None),
        P(None, filt, None),
        P(filt),
    )
    out_specs = (P(filt, SPACE, None, None), P(None, filt, SPACE))
    return jax.shard_map(
        on_device, mesh=fine, in_specs=in_specs, out_specs=out_specs, check_vma=False
    )
```

```python
import math

import jax
import jax.numpy as jnp
from jax import lax
from jax.experimental import pallas as pl
from jax.experimental.pallas import tpu as pltpu
from jax.sharding import Mesh
from jax.sharding import PartitionSpec as P

SPACE = ("x", "zh", "core")
ROWS = 4
DEPTH = 8
WIDTH = 128
STEPS = 8
SCALE = 1.0 / math.sqrt(256 * DEPTH * WIDTH)


def fill(rows, place, blocks, edges):
    zl = place[1]
    for p, block in enumerate(blocks):
        rows[p, pl.ds(1 - zl, 5)] = block[...]
    rows[0:5, 5 * zl] = edges[0]
    rows[5:8, 5 * zl] = edges[1]


def cells_of(rows, row):
    return jnp.concatenate(
        [
            jnp.concatenate(
                [rows[p, row + dx, z] for dx in range(3) for p in range(STEPS)], axis=0
            )
            for z in range(DEPTH)
        ],
        axis=1,
    )


def forward_kernel(place, *refs):
    *blocks, near, far, weights, feat, rows = refs
    y = place[0]
    fill(rows, place, blocks, (near[...], far[...]))
    lane = lax.broadcasted_iota(jnp.int32, (16, WIDTH), 1)
    turned = pltpu.roll(
        weights[...].astype(jnp.float32).reshape(27 * 16, 128), lax.rem(128 - 16 * y + 32, 128), 1
    ).astype(jnp.bfloat16)
    taps = jnp.concatenate(
        [
            jnp.concatenate(
                [turned[16 * (9 * dx + q) : 16 * (9 * dx + q) + 16] for q in range(9)], axis=0
            )
            for dx in range(3)
        ],
        axis=1,
    )
    for row in range(ROWS):
        part = jnp.dot(taps, cells_of(rows, row), preferred_element_type=jnp.float32)
        for z in range(DEPTH):
            sums = []
            for dy in range(3):
                acc = None
                for dz in range(3):
                    if 0 <= z + dz - 1 < DEPTH:
                        at = 16 * (3 * dz + dy)
                        lo = WIDTH * (z + dz - 1)
                        term = part[at : at + 16, lo : lo + WIDTH]
                        acc = term if acc is None else acc + term
                sums.append(acc)
            left = jnp.where(lane == 0, 0.0, pltpu.roll(sums[0], 1, 1))
            right = jnp.where(lane == WIDTH - 1, 0.0, pltpu.roll(sums[2], WIDTH - 1, 1))
            feat[:, row, z, :] = sums[1] + left + right


def shifted(cot, row):
    lane = lax.broadcasted_iota(jnp.int32, (16, WIDTH), 1)
    gap = jnp.zeros((56, WIDTH), jnp.float32)
    empty = jnp.zeros((16, WIDTH), jnp.float32)
    moved = []
    for z in range(DEPTH):
        here = cot[row, z].astype(jnp.float32)
        ahead = jnp.where(lane == WIDTH - 1, 0.0, pltpu.roll(here, WIDTH - 1, 1))
        behind = jnp.where(lane == 0, 0.0, pltpu.roll(here, 1, 1))
        moved.append((ahead, here, behind))
    columns = []
    for z in range(DEPTH):
        column = []
        for half in range(2):
            for dz in range(3):
                for dy in range(3):
                    at = z - dz + 1
                    tile = moved[at][dy] if 0 <= at < DEPTH else empty
                    column.append(tile[8 * half : 8 * half + 8])
            column.append(gap)
        columns.append(jnp.concatenate(column, axis=0).astype(jnp.bfloat16))
    return jnp.concatenate(columns, axis=1)


def edge_cells(near, far):
    return jnp.concatenate(
        [
            jnp.concatenate(
                [near[p, z] for p in range(5)] + [far[p, z] for p in range(3)], axis=0
            )
            for z in range(DEPTH)
        ],
        axis=1,
    )


def over_cells(a, b):
    return lax.dot_general(a, b, (((1,), (1,)), ((), ())), preferred_element_type=jnp.float32)


def receivers(place, half):
    y, zl = place[0], place[1]
    base = lax.rem(zl + half, 2)
    return [base + lax.rem(y + k // 2 + 6, STEPS) * 8 + 4 * (k % 2) for k in range(16)]


def pair_of(one, two, k):
    sub = lax.broadcasted_iota(jnp.int32, (8, WIDTH), 0)
    a, b = one[8 * k : 8 * k + 8], two[8 * k : 8 * k + 8]
    return jnp.where(sub < 4, a, pltpu.roll(b, 4, 0)), jnp.where(sub < 4, pltpu.roll(a, 4, 0), b)


def gradient_kernel(place, *refs):
    *blocks, cot, grad, moved, rows = refs
    zeros = [jnp.zeros((count, DEPTH, 16, WIDTH), jnp.bfloat16) for count in (5, 3)]
    fill(rows, place, blocks, zeros)
    total = jnp.zeros((384, 256), jnp.float32)
    for row in range(ROWS):
        here = shifted(cot, row)
        if row in (0, 3):
            moved[row // 3] = here
        total = total + over_cells(cells_of(rows, row), here)
    wide = lax.broadcasted_iota(jnp.int32, (128, WIDTH), 1)
    for half in range(2):
        one, two, three = (
            total[128 * dx : 128 * dx + 128, WIDTH * half : WIDTH * half + WIDTH]
            for dx in range(3)
        )
        one = jnp.where(wide < 72, one, pltpu.roll(three, 72, 1))
        two = jnp.where(wide < 72, two, pltpu.roll(three, 32, 1))
        for k, at in enumerate(receivers(place, half)):
            grad[at], grad[at + 2] = pair_of(one, two, k)


def edge_kernel(place, near, far, moved, earlier, grad):
    zl = place[1]
    total = over_cells(edge_cells(near, far), moved[zl])
    wide = lax.broadcasted_iota(jnp.int32, (128, WIDTH), 1)
    low = zl == 0
    for half in range(2):
        part = total[:, WIDTH * half : WIDTH * half + WIDTH]
        one = jnp.where(low, part, jnp.where(wide < 72, 0.0, pltpu.roll(part, 72, 1)))
        two = jnp.where(
            jnp.logical_or(low, wide < 72), 0.0, pltpu.roll(part, 32, 1)
        )
        for k, at in enumerate(receivers(place, half)):
            first, second = pair_of(one, two, k)
            grad[at] = earlier[at] + first
            grad[at + 2] = earlier[at + 2] + second


def finish_kernel(place, got, out, turned, table):
    turned[...] = jnp.transpose(jnp.sum(got[...], axis=0) * SCALE)
    for o in range(8):
        for at, count, lane, start in ((0, 9, 0, 0), (9, 9, 4, 0), (18, 5, 0, 72), (23, 4, 4, 72)):
            part = turned[pl.ds(start + o, count, stride=8), :]
            table[at : at + count, 4 * o : 4 * o + 4] = part[:, lane : lane + 4]
    done = jnp.transpose(table[...])
    for o in range(8):
        out[o] = done[4 * o : 4 * o + 4, :27]


def on_device(activations, cotangent, filters, bias_terms):
    y, zl = lax.axis_index("y"), lax.axis_index("zl")
    acts = jnp.transpose(activations, (1, 2, 0, 3))
    cots = jnp.transpose(cotangent, (1, 2, 0, 3))
    first = zl == 0

    swap = [(0, 1), (1, 0)]
    other = lax.ppermute(lax.dynamic_slice_in_dim(acts, 3 * (1 - zl), 5, 0), "zl", swap)
    own = lax.dynamic_slice_in_dim(acts, 3 * zl, 5, 0)
    pairs = []
    for step in range(31):
        pairs += [(32 + step, step + 1), (step + 1, 32 + step)]

    mine = jnp.where(
        first,
        jnp.concatenate([own, other], axis=2),
        jnp.concatenate([other, own], axis=2),
    )
    give = jnp.concatenate(
        [lax.dynamic_slice_in_dim(cots, 4 * (1 - zl), 4, 0).reshape(32, 8, WIDTH), filters], axis=0
    )
    got = lax.ppermute(give, "zl", swap)

    def along(block, by):
        return lax.ppermute(block, "y", [(i, (i - by) % STEPS) for i in range(STEPS)])

    b2, b6 = along(mine, 2), along(mine, -2)
    keep = lax.dynamic_slice_in_dim(cots, 4 * zl, 4, 0)
    cot = jnp.concatenate([keep, got[:32].reshape(4, 8, 8, WIDTH)], axis=2)
    weights = jnp.concatenate([filters, got[32:]], axis=1)
    after, cot, weights = lax.optimization_barrier((mine, cot, weights))
    b1, b7 = along(after, 1), along(after, -1)
    turn = [
        ((2 * i + c), (2 * ((i + (2 if c else -2)) % STEPS) + c))
        for i in range(STEPS)
        for c in range(2)
    ]
    b4 = lax.ppermute(jnp.where(lax.axis_index("core") == 0, b2, b6), ("y", "core"), turn)
    b3, b5 = along(b2, 1), along(b6, -1)

    def outermost(blocks):
        return jnp.stack([jnp.where(first, block[0], block[4]) for block in blocks])

    near = (b6, b7, mine, b1, b2)
    send, b4 = lax.optimization_barrier((outermost(near), b4))
    far = (b3, b4, b5)
    edges = (
        lax.ppermute(send, ("zl",) + SPACE, pairs),
        lax.ppermute(outermost(far), ("zl",) + SPACE, pairs),
    )
    blocks = near + far
    cot, first_edges = lax.optimization_barrier((cot, edges[0]))
    edges = (first_edges, edges[1])

    place = jnp.stack([y, zl])

    def local(kernel, shapes, operands, scratch):
        vmem = pl.BlockSpec(memory_space=pltpu.VMEM)
        return pl.pallas_call(
            kernel,
            out_shape=shapes,
            in_specs=[pl.BlockSpec(memory_space=pltpu.SMEM)] + [vmem] * len(operands),
            out_specs=jax.tree.map(lambda _: vmem, shapes),
            scratch_shapes=scratch,
            compiler_params=pltpu.CompilerParams(vmem_limit_bytes=48 * 1024 * 1024),
            cost_estimate=pl.CostEstimate(
                flops=10**8 * len(operands), bytes_accessed=3 * 10**6, transcendentals=0
            ),
        )(place, *operands)

    tiles = jax.ShapeDtypeStruct((64, 8, WIDTH), jnp.float32)
    rows = [pltpu.VMEM((STEPS, 6, DEPTH, 16, WIDTH), jnp.bfloat16)]
    grad, moved = local(
        gradient_kernel,
        (tiles, jax.ShapeDtypeStruct((2, 256, DEPTH * WIDTH), jnp.bfloat16)),
        (*blocks, cot),
        rows,
    )
    grad = local(edge_kernel, tiles, (*edges, moved, grad), [])
    weights, grad = lax.optimization_barrier((weights, grad))
    feat = local(
        forward_kernel,
        jax.ShapeDtypeStruct((16, ROWS, DEPTH, WIDTH), jnp.float32),
        (*blocks, *edges, weights),
        rows,
    )

    got = lax.all_to_all(grad, SPACE + ("zl",), 0, 0, tiled=True)
    filter_grad = local(
        finish_kernel,
        jax.ShapeDtypeStruct((8, 4, 27), jnp.float32),
        (got,),
        [pltpu.VMEM((WIDTH, 8), jnp.float32), pltpu.VMEM((32, WIDTH), jnp.float32)],
    ).transpose(2, 0, 1)

    rest = lax.ppermute(feat[8:], "zl", swap)
    kept = feat[:8]
    features_out = jnp.where(
        first,
        jnp.concatenate([kept, rest], axis=1),
        jnp.concatenate([rest, kept], axis=1),
    ) + bias_terms.astype(jnp.float32)[:, None, None, None]
    return (features_out, filter_grad)


def solution(mesh):
    fine = Mesh(mesh.devices.reshape(8, 2, 4, 4, 2), ("y", "zl", "x", "zh", "core"))
    filt = ("y", "zl")
    in_specs = (
        P(filt, SPACE, None, None),
        P(filt, SPACE, None, None),
        P(None, filt, None),
        P(filt),
    )
    out_specs = (P(filt, SPACE, None, None), P(None, filt, SPACE))
    return jax.shard_map(
        on_device, mesh=fine, in_specs=in_specs, out_specs=out_specs, check_vma=False
    )
```

```python
import math

import jax
import jax.numpy as jnp
from jax import lax
from jax.experimental import pallas as pl
from jax.experimental.pallas import tpu as pltpu
from jax.sharding import Mesh
from jax.sharding import PartitionSpec as P

SPACE = ("x", "zh", "core")
ROWS = 4
DEPTH = 8
WIDTH = 128
STEPS = 8
SCALE = 1.0 / math.sqrt(256 * DEPTH * WIDTH)


def fill(rows, place, blocks, edges):
    zl = place[1]
    for p, block in enumerate(blocks):
        rows[p, pl.ds(1 - zl, 5)] = block[...]
    rows[0:5, 5 * zl] = edges[0]
    rows[5:8, 5 * zl] = edges[1]


def cells_of(rows, row):
    return jnp.concatenate(
        [
            jnp.concatenate(
                [rows[p, row + dx, z] for dx in range(3) for p in range(STEPS)], axis=0
            )
            for z in range(DEPTH)
        ],
        axis=1,
    )


def forward_kernel(place, *refs):
    *blocks, near, far, weights, feat, rows = refs
    y = place[0]
    fill(rows, place, blocks, (near[...], far[...]))
    lane = lax.broadcasted_iota(jnp.int32, (16, WIDTH), 1)
    turned = pltpu.roll(
        weights[...].astype(jnp.float32).reshape(27 * 16, 128), lax.rem(128 - 16 * y + 32, 128), 1
    ).astype(jnp.bfloat16)
    taps = jnp.concatenate(
        [
            jnp.concatenate(
                [turned[16 * (9 * dx + q) : 16 * (9 * dx + q) + 16] for q in range(9)], axis=0
            )
            for dx in range(3)
        ],
        axis=1,
    )
    for row in range(ROWS):
        part = jnp.dot(taps, cells_of(rows, row), preferred_element_type=jnp.float32)
        for z in range(DEPTH):
            sums = []
            for dy in range(3):
                acc = None
                for dz in range(3):
                    if 0 <= z + dz - 1 < DEPTH:
                        at = 16 * (3 * dz + dy)
                        lo = WIDTH * (z + dz - 1)
                        term = part[at : at + 16, lo : lo + WIDTH]
                        acc = term if acc is None else acc + term
                sums.append(acc)
            left = jnp.where(lane == 0, 0.0, pltpu.roll(sums[0], 1, 1))
            right = jnp.where(lane == WIDTH - 1, 0.0, pltpu.roll(sums[2], WIDTH - 1, 1))
            feat[:, row, z, :] = sums[1] + left + right


def shifted(cot, row):
    lane = lax.broadcasted_iota(jnp.int32, (16, WIDTH), 1)
    gap = jnp.zeros((56, WIDTH), jnp.float32)
    empty = jnp.zeros((16, WIDTH), jnp.float32)
    moved = []
    for z in range(DEPTH):
        here = cot[row, z].astype(jnp.float32)
        ahead = jnp.where(lane == WIDTH - 1, 0.0, pltpu.roll(here, WIDTH - 1, 1))
        behind = jnp.where(lane == 0, 0.0, pltpu.roll(here, 1, 1))
        moved.append((ahead, here, behind))
    columns = []
    for z in range(DEPTH):
        column = []
        for half in range(2):
            for dz in range(3):
                for dy in range(3):
                    at = z - dz + 1
                    tile = moved[at][dy] if 0 <= at < DEPTH else empty
                    column.append(tile[8 * half : 8 * half + 8])
            column.append(gap)
        columns.append(jnp.concatenate(column, axis=0).astype(jnp.bfloat16))
    return jnp.concatenate(columns, axis=1)


def edge_cells(near, far):
    return jnp.concatenate(
        [
            jnp.concatenate(
                [near[p, z] for p in range(5)] + [far[p, z] for p in range(3)], axis=0
            )
            for z in range(DEPTH)
        ],
        axis=1,
    )


def over_cells(a, b):
    return lax.dot_general(a, b, (((1,), (1,)), ((), ())), preferred_element_type=jnp.float32)


def receivers(place, half):
    y, zl = place[0], place[1]
    base = lax.rem(zl + half, 2)
    return [base + lax.rem(y + k // 2 + 6, STEPS) * 8 + 4 * (k % 2) for k in range(16)]


def pair_of(one, two, k):
    sub = lax.broadcasted_iota(jnp.int32, (8, WIDTH), 0)
    a, b = one[8 * k : 8 * k + 8], two[8 * k : 8 * k + 8]
    return jnp.where(sub < 4, a, pltpu.roll(b, 4, 0)), jnp.where(sub < 4, pltpu.roll(a, 4, 0), b)


def gradient_kernel(place, *refs):
    *blocks, cot, grad, moved, rows = refs
    zeros = [jnp.zeros((count, DEPTH, 16, WIDTH), jnp.bfloat16) for count in (5, 3)]
    fill(rows, place, blocks, zeros)
    total = jnp.zeros((384, 256), jnp.float32)
    for row in range(ROWS):
        here = shifted(cot, row)
        if row in (0, 3):
            moved[row // 3] = here
        total = total + over_cells(cells_of(rows, row), here)
    wide = lax.broadcasted_iota(jnp.int32, (128, WIDTH), 1)
    for half in range(2):
        one, two, three = (
            total[128 * dx : 128 * dx + 128, WIDTH * half : WIDTH * half + WIDTH]
            for dx in range(3)
        )
        one = jnp.where(wide < 72, one, pltpu.roll(three, 72, 1))
        two = jnp.where(wide < 72, two, pltpu.roll(three, 32, 1))
        for k, at in enumerate(receivers(place, half)):
            grad[at], grad[at + 2] = pair_of(one, two, k)


def edge_kernel(place, near, far, moved, earlier, grad):
    zl = place[1]
    total = over_cells(edge_cells(near, far), moved[zl])
    wide = lax.broadcasted_iota(jnp.int32, (128, WIDTH), 1)
    low = zl == 0
    for half in range(2):
        part = total[:, WIDTH * half : WIDTH * half + WIDTH]
        one = jnp.where(low, part, jnp.where(wide < 72, 0.0, pltpu.roll(part, 72, 1)))
        two = jnp.where(
            jnp.logical_or(low, wide < 72), 0.0, pltpu.roll(part, 32, 1)
        )
        for k, at in enumerate(receivers(place, half)):
            first, second = pair_of(one, two, k)
            grad[at] = earlier[at] + first
            grad[at + 2] = earlier[at + 2] + second


def finish_kernel(place, got, out, turned, table):
    turned[...] = jnp.transpose(jnp.sum(got[...], axis=0) * SCALE)
    for o in range(8):
        for at, count, lane, start in ((0, 9, 0, 0), (9, 9, 4, 0), (18, 5, 0, 72), (23, 4, 4, 72)):
            part = turned[pl.ds(start + o, count, stride=8), :]
            table[at : at + count, 4 * o : 4 * o + 4] = part[:, lane : lane + 4]
    done = jnp.transpose(table[...])
    for o in range(8):
        out[o] = done[4 * o : 4 * o + 4, :27]


def on_device(activations, cotangent, filters, bias_terms):
    y, zl = lax.axis_index("y"), lax.axis_index("zl")
    acts = jnp.transpose(activations, (1, 2, 0, 3))
    cots = jnp.transpose(cotangent, (1, 2, 0, 3))
    first = zl == 0

    swap = [(0, 1), (1, 0)]
    other = lax.ppermute(lax.dynamic_slice_in_dim(acts, 3 * (1 - zl), 5, 0), "zl", swap)
    own = lax.dynamic_slice_in_dim(acts, 3 * zl, 5, 0)
    pairs = []
    for step in range(31):
        pairs += [(32 + step, step + 1), (step + 1, 32 + step)]

    mine = jnp.where(
        first,
        jnp.concatenate([own, other], axis=2),
        jnp.concatenate([other, own], axis=2),
    )
    give = jnp.concatenate(
        [lax.dynamic_slice_in_dim(cots, 4 * (1 - zl), 4, 0).reshape(32, 8, WIDTH), filters], axis=0
    )
    got = lax.ppermute(give, "zl", swap)

    def along(block, by):
        return lax.ppermute(block, "y", [(i, (i - by) % STEPS) for i in range(STEPS)])

    b2, b6 = along(mine, 2), along(mine, -2)
    keep = lax.dynamic_slice_in_dim(cots, 4 * zl, 4, 0)
    cot = jnp.concatenate([keep, got[:32].reshape(4, 8, 8, WIDTH)], axis=2)
    weights = jnp.concatenate([filters, got[32:]], axis=1)
    after, cot, weights = lax.optimization_barrier((mine, cot, weights))
    b1, b7 = along(after, 1), along(after, -1)
    turn = [
        ((2 * i + c), (2 * ((i + (2 if c else -2)) % STEPS) + c))
        for i in range(STEPS)
        for c in range(2)
    ]
    b4 = lax.ppermute(jnp.where(lax.axis_index("core") == 0, b2, b6), ("y", "core"), turn)
    b3, b5 = along(b2, 1), along(b6, -1)

    def outermost(blocks):
        return jnp.stack([jnp.where(first, block[0], block[4]) for block in blocks])

    near = (b6, b7, mine, b1, b2)
    send, b4 = lax.optimization_barrier((outermost(near), b4))
    far = (b3, b4, b5)
    edges = (
        lax.ppermute(send, ("zl",) + SPACE, pairs),
        lax.ppermute(outermost(far), ("zl",) + SPACE, pairs),
    )
    blocks = near + far
    cot, first_edges = lax.optimization_barrier((cot, edges[0]))
    edges = (first_edges, edges[1])

    place = jnp.stack([y, zl])

    def local(kernel, shapes, operands, scratch):
        vmem = pl.BlockSpec(memory_space=pltpu.VMEM)
        return pl.pallas_call(
            kernel,
            out_shape=shapes,
            in_specs=[pl.BlockSpec(memory_space=pltpu.SMEM)] + [vmem] * len(operands),
            out_specs=jax.tree.map(lambda _: vmem, shapes),
            scratch_shapes=scratch,
            compiler_params=pltpu.CompilerParams(vmem_limit_bytes=48 * 1024 * 1024),
            cost_estimate=pl.CostEstimate(
                flops=10**8 * len(operands), bytes_accessed=3 * 10**6, transcendentals=0
            ),
        )(place, *operands)

    tiles = jax.ShapeDtypeStruct((64, 8, WIDTH), jnp.float32)
    rows = [pltpu.VMEM((STEPS, 6, DEPTH, 16, WIDTH), jnp.bfloat16)]
    grad, moved = local(
        gradient_kernel,
        (tiles, jax.ShapeDtypeStruct((2, 256, DEPTH * WIDTH), jnp.bfloat16)),
        (*blocks, cot),
        rows,
    )
    grad = local(edge_kernel, tiles, (*edges, moved, grad), [])
    weights, grad = lax.optimization_barrier((weights, grad))
    feat = local(
        forward_kernel,
        jax.ShapeDtypeStruct((16, ROWS, DEPTH, WIDTH), jnp.float32),
        (*blocks, *edges, weights),
        rows,
    )

    got = lax.all_to_all(grad, SPACE + ("zl",), 0, 0, tiled=True)
    filter_grad = local(
        finish_kernel,
        jax.ShapeDtypeStruct((8, 4, 27), jnp.float32),
        (got,),
        [pltpu.VMEM((WIDTH, 8), jnp.float32), pltpu.VMEM((32, WIDTH), jnp.float32)],
    ).transpose(2, 0, 1)

    rest = lax.ppermute(feat[8:], "zl", swap)
    rest, filter_grad = lax.optimization_barrier((rest, filter_grad))
    kept = feat[:8]
    features_out = jnp.where(
        first,
        jnp.concatenate([kept, rest], axis=1),
        jnp.concatenate([rest, kept], axis=1),
    ) + bias_terms.astype(jnp.float32)[:, None, None, None]
    return (features_out, filter_grad)


def solution(mesh):
    fine = Mesh(mesh.devices.reshape(8, 2, 4, 4, 2), ("y", "zl", "x", "zh", "core"))
    filt = ("y", "zl")
    in_specs = (
        P(filt, SPACE, None, None),
        P(filt, SPACE, None, None),
        P(None, filt, None),
        P(filt),
    )
    out_specs = (P(filt, SPACE, None, None), P(None, filt, SPACE))
    return jax.shard_map(
        on_device, mesh=fine, in_specs=in_specs, out_specs=out_specs, check_vma=False
    )
```
